256 devices in a mesh: wave: 32 (over z, x_lo, core), rows: 8 (over y, x_hi).
Axes of the slice: x: 4 (x_hi: 2, x_lo: 2; x = x_hi * 2 + x_lo), y: 4, z: 8, core: 2. Of those that a mesh axis runs over, the one named last changes fastest.
Arguments:
- potential: bfloat16 [4, 512, 2048], P(None, 'rows', 'wave'), may hold values from 0 to 1
- tilt_index: int32 [64, 2], P('wave'), may hold values from -128 to 127
Outputs:
- exit_wave: bfloat16 [2, 64, 512, 2048], P(None, 'wave', 'rows')
The draws below stay inside these ranges and needn't reach their ends.
All inputs are finite; a program needn't handle non-finite values.
Results may differ from the reference program's by a relative error of at most 0.025.
Values may be sent and summed in bfloat16 or wider, within the bound.
No kernel may reach another device: no remote copies, remote signals or barrier semaphores. Data moves between devices by JAX's collectives and lax.ppermute only.
A program may use at most 64 MiB of HBM per device.

```python
import math
import jax
import jax.numpy as jnp
from jax import lax

NX = 2048
TAPS = 33
BLOCK = 128
SLICES = 4
ROWS_DEV = 64
NY = 512
WAVES = 64


def touch_ends(drawn, rng, low, top_value):
    longest = drawn.shape.index(max(drawn.shape))
    spots = []
    for shift in (0, 1):
        where = [jax.random.randint(jax.random.fold_in(rng, axis), (), 0, length) for axis, length in enumerate(drawn.shape)]
        where[longest] = (where[longest] + shift) % drawn.shape[longest]
        spots.append(tuple(where))
    return drawn.at[spots[0]].set(low).at[spots[1]].set(top_value)


def level_of(key, shape, split, smallest, top_value):
    factor_of, own = 1.0, jax.random.fold_in(key, 6)
    for position, blocks in split:
        heights = jnp.exp(jax.random.uniform(jax.random.fold_in(own, position), (blocks,), jnp.float32, smallest / len(split), top_value / len(split)))
        factor_of = factor_of * jnp.repeat(heights, shape[position] // blocks).reshape([-1 if axis == position else 1 for axis in range(len(shape))])
    return factor_of


def setup_inputs(seed: int = 0) -> dict:
    arg_keys = jax.random.split(jax.random.key(seed), 3)
    potential = jnp.clip(1.0 * jax.random.uniform(arg_keys[0], (SLICES, NY, NX), jnp.float32) ** level_of(arg_keys[0], (SLICES, NY, NX), ((1, 8), (2, 32)), -0.2, 0.2), 0.0, 1.0).astype(jnp.bfloat16)
    tilt_index = touch_ends(jax.random.randint(arg_keys[1], (WAVES, 2), -128, 128), jax.random.fold_in(arg_keys[1], 1), -128, 127).astype(jnp.int32)
    return dict(potential=potential, tilt_index=tilt_index)


def band_kernel(width):
    reach = TAPS // 2
    inner = jnp.arange(width + 2 * reach)[:, None]
    outer = jnp.arange(width)[None, :]
    offset = inner - outer
    valid = (offset >= 0) & (offset < TAPS)
    centred = (offset - reach).astype(jnp.float32)
    angle_val = math.pi * centred * centred / TAPS
    weight = jnp.where(valid, 1.0 / math.sqrt(TAPS), 0.0).astype(jnp.float32)
    real_part = (jnp.cos(angle_val) * weight).astype(jnp.bfloat16)
    imag_part = (jnp.sin(angle_val) * weight).astype(jnp.bfloat16)
    return jnp.stack([jnp.stack([real_part, imag_part]), jnp.stack([-imag_part, real_part])])

def column_pass(field, kernel):
    reach = TAPS // 2
    padded = jnp.pad(field, ((0, 0), (0, 0), (reach, reach)))
    count = field.shape[2] // BLOCK
    windows = jnp.stack([padded[:, :, b * BLOCK:b * BLOCK + BLOCK + 2 * reach] for b in range(count)], axis=2)
    result = jnp.einsum('prbm,pqmc->qrbc', windows.astype(jnp.float32), kernel.astype(jnp.float32))
    return result.reshape(field.shape)

def row_pass(padded, kernel, row_block):
    reach = TAPS // 2
    total = padded.shape[1] - 2 * reach
    count = total // row_block
    windows = jnp.stack([padded[:, b * row_block:b * row_block + row_block + 2 * reach, :] for b in range(count)], axis=1)
    result = jnp.einsum('pbmc,pqmr->qbrc', windows.astype(jnp.float32), kernel.astype(jnp.float32))
    return result.reshape((2, total, padded.shape[2]))

def reference(potential, tilt_index):
    reach = TAPS // 2
    row_block = min(BLOCK, ROWS_DEV)
    col_kernel = band_kernel(BLOCK)
    row_kernel = band_kernel(row_block)
    phase_val = 3.0 * potential.astype(jnp.float32)
    trans_re = jnp.cos(phase_val).astype(jnp.bfloat16)
    trans_im = jnp.sin(phase_val).astype(jnp.bfloat16)
    y_index = jnp.arange(NY, dtype=jnp.int32)
    x_index = jnp.arange(NX, dtype=jnp.int32)

    def one_wave(tilt):
        y_turn = (tilt[0] * y_index % NY).astype(jnp.float32) / NY
        x_turn = (tilt[1] * x_index % NX).astype(jnp.float32) / NX
        angle_val = 2.0 * math.pi * (y_turn[:, None] + x_turn[None, :])
        wave = jnp.stack([jnp.cos(angle_val), jnp.sin(angle_val)]).astype(jnp.bfloat16)
        for slice_num in range(SLICES):
            wave_re = wave[0].astype(jnp.float32)
            wave_im = wave[1].astype(jnp.float32)
            t_re = trans_re[slice_num].astype(jnp.float32)
            t_im = trans_im[slice_num].astype(jnp.float32)
            moved = jnp.stack([wave_re * t_re - wave_im * t_im, wave_re * t_im + wave_im * t_re]).astype(jnp.bfloat16)
            half_step = column_pass(moved, col_kernel).astype(jnp.bfloat16)
            padded = jnp.pad(half_step, ((0, 0), (reach, reach), (0, 0)))
            wave = row_pass(padded, row_kernel, row_block).astype(jnp.bfloat16)
        return wave
    waves_out = lax.map(one_wave, tilt_index)
    return jnp.transpose(waves_out, (1, 0, 2, 3))
```

```python
import functools
import math

import jax
import jax.numpy as jnp
import numpy as np
from jax import lax
from jax.experimental import pallas as pl
from jax.experimental.pallas import tpu as pltpu
from jax.sharding import PartitionSpec as P

NX = 2048
NY = 512
TAPS = 33
REACH = TAPS // 2
SLICES = 4
ROWS = 64
LANES = 128
BLOCKS = NX // LANES
ZS, WAVE, RANKS = 8, 32, 8
HALO = [REACH * (SLICES - s) for s in range(SLICES)]
IN_ROWS = [ROWS + 2 * h for h in HALO]
HALF = [n // 2 for n in IN_ROWS]
HALF_AT = [sum(HALF[:s]) for s in range(SLICES)]
HALF_ALL = sum(HALF)
BOTH = ("wave", "rows")


def place(z, lo, core, rank):
    return ((z * 2 + lo) * 2 + core) * RANKS + rank


def send(value, target_of):
    pairs = []
    for z in range(ZS):
        for lo in range(2):
            for core in range(2):
                for rank in range(RANKS):
                    target = target_of(z, lo, core, rank)
                    if target is not None:
                        pairs.append((place(z, lo, core, rank), place(*target)))
    return lax.ppermute(value, BOTH, pairs)


def to_core(z, lo, core, rank):
    return z, lo, 1 - core, rank


def to_pair(z, lo, core, rank):
    return z, 1 - lo, core, rank


def to_rank(z, lo, core, rank):
    rank += 1 - 2 * core
    return (z, lo, core, rank) if 0 <= rank < RANKS else None


def to_rank_pair(z, lo, core, rank):
    target = to_rank(z, lo, core, rank)
    return None if target is None else to_pair(*target)


def to_up(z, lo, core, rank):
    return (z + 1) % ZS, lo, core, rank


def to_down(z, lo, core, rank):
    return (z - 1) % ZS, lo, core, rank


def taps():
    d = np.arange(TAPS, dtype=np.float32) - REACH
    angle = np.float32(math.pi) * d * d / TAPS
    scale = np.float32(1.0 / math.sqrt(TAPS))
    return np.cos(angle) * scale, np.sin(angle) * scale


def band(inside, outside, shift):
    at = np.arange(inside)[:, None] - np.arange(outside)[None, :] + shift
    valid = (at >= 0) & (at < TAPS)
    at = np.clip(at, 0, TAPS - 1)
    return tuple(np.where(valid, part[at], np.float32(0.0)) for part in taps())


def column_weights():
    def packed(re, im):
        return np.block([[re, im], [-im, re]])

    middle = band(LANES, LANES, REACH)
    left = band(LANES, LANES, REACH - LANES)
    right = band(LANES, LANES, REACH + LANES)
    return np.stack([packed(*middle), packed(left[0] + right[0], left[1] + right[1])])


def polynomial(func, degree):
    w = 0.125 * (1.0 + np.cos(np.pi * (np.arange(64) + 0.5) / 64))
    fit = np.polynomial.chebyshev.Chebyshev.fit(w, func(3.0 * np.sqrt(w)), degree, domain=[0.0, 0.25])
    return [float(c) for c in fit.convert(kind=np.polynomial.Polynomial).coef]


EVEN = polynomial(np.cos, 4)
ODD = polynomial(lambda x: np.sin(x) / (x / 3.0), 4)


def horner(coefs, w):
    total = jnp.full_like(w, coefs[-1])
    for c in coefs[-2::-1]:
        total = total * w + c
    return total


def cosine_sine(tile):
    v = tile - 0.5
    w = v * v
    cos_v, sin_v = horner(EVEN, w), horner(ODD, w) * v
    c, s = math.cos(1.5), math.sin(1.5)
    return cos_v * c - sin_v * s, cos_v * s + sin_v * c


def body(where_ref, *refs):
    mine, other = refs[:ZS], refs[ZS : 2 * ZS]
    weights, rows_band = refs[2 * ZS], refs[2 * ZS + 1 : 2 * ZS + 1 + SLICES]
    x_wave, y_wave, out = refs[2 * ZS + 1 + SLICES : 2 * ZS + 4 + SLICES]
    trans = refs[2 * ZS + 4 + SLICES : 2 * ZS + 4 + 2 * SLICES]
    fields = refs[2 * ZS + 4 + 2 * SLICES :]
    z0, core = where_ref[0], where_ref[1]

    for field in fields:
        for edge in (0, BLOCKS + 1):
            field[edge] = jnp.zeros(field.shape[1:], field.dtype)

    for k in range(ZS):
        base = lax.rem(z0 + k, ZS) * 2
        for ref, side in ((mine[k], core), (other[k], 1 - core)):
            for s in range(SLICES):

                def convert(lo, carry, ref=ref, side=side, s=s, base=base):
                    tile = ref[lo, HALF_AT[s] : HALF_AT[s] + HALF[s], :].astype(jnp.float32)
                    re, im = cosine_sine(tile)
                    at = pl.ds(pl.multiple_of(side * HALF[s], 16), HALF[s])
                    trans[s][base + lo, at, 0:LANES] = re.astype(jnp.bfloat16)
                    trans[s][base + lo, at, LANES:] = im.astype(jnp.bfloat16)
                    return carry

                lax.fori_loop(0, 2, convert, 0)

    def times(re, im, t):
        t_re = t[:, :LANES].astype(jnp.float32)
        t_im = t[:, LANES:].astype(jnp.float32)
        return (re * t_re - im * t_im).astype(jnp.bfloat16), (re * t_im + im * t_re).astype(jnp.bfloat16)

    def begin(b, carry):
        for wv in range(2):
            x_re, x_im = x_wave[b, wv, 0:1, :], x_wave[b, wv, 1:2, :]
            y_re, y_im = y_wave[wv, 0], y_wave[wv, 1]
            re, im = x_re * y_re - x_im * y_im, x_re * y_im + x_im * y_re
            re, im = times(re, im, trans[0][b])
            fields[0][b + 1, wv, 0 : IN_ROWS[0], 0:LANES] = re
            fields[0][b + 1, wv, 0 : IN_ROWS[0], LANES:] = im
        return carry

    lax.fori_loop(0, BLOCKS, begin, 0)

    for s in range(SLICES):
        rows_in, rows_out = IN_ROWS[s], IN_ROWS[s] - 2 * REACH
        here, there = fields[s % 2], fields[(s + 1) % 2]

        def step(b, carry, s=s, rows_in=rows_in, rows_out=rows_out, here=here, there=there):
            lane = lax.broadcasted_iota(jnp.int32, (rows_in, 2 * LANES), 1)
            from_left = (lane & (LANES - 1)) >= LANES // 2
            for wv in range(2):
                centre = here[b + 1, wv, 0:rows_in, :]
                edges = jnp.where(from_left, here[b, wv, 0:rows_in, :], here[b + 2, wv, 0:rows_in, :])
                half = jnp.dot(centre, weights[0], preferred_element_type=jnp.float32)
                half += jnp.dot(edges, weights[1], preferred_element_type=jnp.float32)
                both = jnp.dot(rows_band[s][...], half.astype(jnp.bfloat16), preferred_element_type=jnp.float32)
                re = both[:rows_out, :LANES] - both[rows_out:, LANES:]
                im = both[rows_out:, :LANES] + both[:rows_out, LANES:]
                if s + 1 < SLICES:
                    re, im = times(re, im, trans[s + 1][b])
                    there[b + 1, wv, 0:rows_out, 0:LANES] = re
                    there[b + 1, wv, 0:rows_out, LANES:] = im
                else:
                    at = pl.ds(pl.multiple_of(b * LANES, LANES), LANES)
                    out[0, wv, :, at] = re.astype(jnp.bfloat16)
                    out[1, wv, :, at] = im.astype(jnp.bfloat16)
            return carry

        lax.fori_loop(0, BLOCKS, step, 0)


def per_device(potential, tilt_index):
    wave_at, rank = lax.axis_index("wave"), lax.axis_index("rows")
    z, lo, core = wave_at // 4, (wave_at // 2) % 2, wave_at % 2

    swapped = send(potential, to_core)
    first = core == 0
    both = jnp.concatenate(
        [jnp.where(first, potential, swapped), jnp.where(first, swapped, potential)], axis=2
    )
    down = jnp.concatenate([both[s, ROWS - HALO[s] :] for s in range(SLICES)], axis=0)
    up = jnp.concatenate([both[s, : HALO[s]] for s in range(SLICES)], axis=0)
    halo_out = jnp.where(first, down, up)
    own = jnp.where(first, both[:, : ROWS // 2], both[:, ROWS // 2 :])
    halo = send(halo_out, to_rank)
    own_pair = send(own, to_pair)
    halo_pair = send(halo_out, to_rank_pair)

    def half_of(own, halo):
        top, bottom = [], []
        for s in range(SLICES):
            at = sum(HALO[:s])
            piece = halo[at : at + HALO[s]]
            top += [piece, own[s]]
            bottom += [own[s], piece]
        return jnp.where(first, jnp.concatenate(top, axis=0), jnp.concatenate(bottom, axis=0))

    here, pair = half_of(own, halo), half_of(own_pair, halo_pair)
    block = jnp.where(lo == 0, jnp.stack([here, pair]), jnp.stack([pair, here]))

    blocks = [block] + [None] * (ZS - 1)
    rising = falling = block
    for k in range(1, ZS // 2 + 1):
        rising = send(rising, to_up)
        blocks[ZS - k] = rising
        if k < ZS // 2:
            falling = send(falling, to_down)
            blocks[k] = falling
    others = [send(value, to_core) for value in blocks]

    y = rank * ROWS - HALO[0] + jnp.arange(IN_ROWS[0], dtype=jnp.int32)
    inside = ((y >= 0) & (y < NY)).astype(jnp.float32)
    turn_y = (tilt_index[:, 0:1] * y[None, :] % NY).astype(jnp.float32) * (2.0 * math.pi / NY)
    y_wave = jnp.stack([jnp.cos(turn_y) * inside, jnp.sin(turn_y) * inside], axis=1)
    y_wave = jnp.broadcast_to(y_wave[..., None], (*y_wave.shape, LANES))
    x = jnp.arange(NX, dtype=jnp.int32)
    turn_x = (tilt_index[:, 1:2] * x[None, :] % NX).astype(jnp.float32) * (2.0 * math.pi / NX)
    x_wave = jnp.stack([jnp.cos(turn_x), jnp.sin(turn_x)], axis=1)
    x_wave = x_wave.reshape(2, 2, BLOCKS, LANES).transpose(2, 0, 1, 3)

    weights = jnp.asarray(column_weights(), jnp.bfloat16)
    rows_band = []
    for s in range(SLICES):
        rows_in, rows_out = IN_ROWS[s], IN_ROWS[s] - 2 * REACH
        re, im = band(rows_in, rows_out, 0)
        stacked = jnp.asarray(np.concatenate([re.T, im.T], axis=0), jnp.bfloat16)
        y_out = rank * ROWS - HALO[s] + REACH + jnp.arange(rows_out, dtype=jnp.int32)
        keep = (y_out >= 0) & (y_out < NY)
        rows_band.append(jnp.where(jnp.concatenate([keep, keep])[:, None], stacked, 0))

    where = jnp.stack([z, core]).astype(jnp.int32)
    vmem = pl.BlockSpec(memory_space=pltpu.VMEM)
    operands = [*blocks, *others, weights, *rows_band, x_wave, y_wave]
    return pl.pallas_call(
        body,
        out_shape=jax.ShapeDtypeStruct((2, 2, ROWS, NX), jnp.bfloat16),
        in_specs=[pl.BlockSpec(memory_space=pltpu.SMEM)] + [vmem] * len(operands),
        out_specs=vmem,
        scratch_shapes=[pltpu.VMEM((BLOCKS, n, 2 * LANES), jnp.bfloat16) for n in IN_ROWS]
        + [pltpu.VMEM((BLOCKS + 2, 2, IN_ROWS[s], 2 * LANES), jnp.bfloat16) for s in range(2)],
        compiler_params=pltpu.CompilerParams(vmem_limit_bytes=40 * 2**20),
        cost_estimate=pl.CostEstimate(flops=10 * 10**9, bytes_accessed=4 * 2**20, transcendentals=0),
    )(where, *operands)


def solution(mesh):
    return jax.shard_map(
        per_device,
        mesh=mesh,
        in_specs=(P(None, "rows", "wave"), P("wave", None)),
        out_specs=P(None, "wave", "rows", None),
        check_vma=False,
    )
```

```python
import functools
import math

import jax
import jax.numpy as jnp
import numpy as np
from jax import lax
from jax.experimental import pallas as pl
from jax.experimental.pallas import tpu as pltpu
from jax.sharding import PartitionSpec as P

NX = 2048
NY = 512
TAPS = 33
REACH = TAPS // 2
SLICES = 4
ROWS = 64
LANES = 128
BLOCKS = NX // LANES
ZS, WAVE, RANKS = 8, 32, 8
HALO = [REACH * (SLICES - s) for s in range(SLICES)]
IN_ROWS = [ROWS + 2 * h for h in HALO]
HALF = [n // 2 for n in IN_ROWS]
HALF_AT = [sum(HALF[:s]) for s in range(SLICES)]
HALF_ALL = sum(HALF)
BOTH = ("wave", "rows")
CORE_ROWS = ROWS // 2
HALO_ALL = sum(HALO)


def place(z, lo, core, rank):
    return ((z * 2 + lo) * 2 + core) * RANKS + rank


def send(value, target_of):
    pairs = []
    for z in range(ZS):
        for lo in range(2):
            for core in range(2):
                for rank in range(RANKS):
                    target = target_of(z, lo, core, rank)
                    if target is not None:
                        pairs.append((place(z, lo, core, rank), place(*target)))
    return lax.ppermute(value, BOTH, pairs)


def to_core(z, lo, core, rank):
    return z, lo, 1 - core, rank


def to_pair(z, lo, core, rank):
    return z, 1 - lo, core, rank


def to_rank(z, lo, core, rank):
    rank += 1 - 2 * core
    return (z, lo, core, rank) if 0 <= rank < RANKS else None


def to_next(z, lo, core, rank):
    return (z + 1 - 2 * core) % ZS, lo, core, rank


def taps():
    d = np.arange(TAPS, dtype=np.float32) - REACH
    angle = np.float32(math.pi) * d * d / TAPS
    scale = np.float32(1.0 / math.sqrt(TAPS))
    return np.cos(angle) * scale, np.sin(angle) * scale


def band(inside, outside, shift):
    at = np.arange(inside)[:, None] - np.arange(outside)[None, :] + shift
    valid = (at >= 0) & (at < TAPS)
    at = np.clip(at, 0, TAPS - 1)
    return tuple(np.where(valid, part[at], np.float32(0.0)) for part in taps())


def column_weights():
    def packed(re, im):
        return np.block([[re, im], [-im, re]])

    middle = band(LANES, LANES, REACH)
    left = band(LANES, LANES, REACH - LANES)
    right = band(LANES, LANES, REACH + LANES)
    return np.concatenate([packed(*middle), packed(left[0] + right[0], left[1] + right[1])])


def row_weights(s):
    re, im = (part.T for part in band(IN_ROWS[s], IN_ROWS[s] - 2 * REACH, 0))
    return np.block([[re, -im], [im, re]])


def polynomial(func, degree):
    w = 0.125 * (1.0 + np.cos(np.pi * (np.arange(64) + 0.5) / 64))
    fit = np.polynomial.chebyshev.Chebyshev.fit(w, func(3.0 * np.sqrt(w)), degree, domain=[0.0, 0.25])
    return [float(c) for c in fit.convert(kind=np.polynomial.Polynomial).coef]


EVEN = polynomial(np.cos, 4)
ODD = polynomial(lambda x: np.sin(x) / (x / 3.0), 4)


def horner(coefs, w):
    total = jnp.full_like(w, coefs[-1])
    for c in coefs[-2::-1]:
        total = total * w + c
    return total


def cosine_sine(tile):
    v = tile - 0.5
    w = v * v
    cos_v, sin_v = horner(EVEN, w), horner(ODD, w) * v
    c, s = math.cos(1.5), math.sin(1.5)
    return cos_v * c - sin_v * s, cos_v * s + sin_v * c


CALLS = (
    (1, ((-1, 4),)),
    (2, ((-3, 2), (3, 2))),
    (3, ((-5, 2), (5, 2))),
    (4, ((7, 4),)),
)


def body(groups, holders, first_call, where_ref, *refs):
    count = sum(n for _, n in groups)
    pieces = refs[: len(holders)]
    weights, rows_band = refs[len(holders)], refs[len(holders) + 1 : len(holders) + 1 + SLICES]
    rest = refs[len(holders) + 1 + SLICES :]
    x_wave, y_wave = rest[:2]
    rest = rest[2 if first_call else 3 :]
    out, trans, fields, made, sems = rest[0], rest[1:SLICES], rest[SLICES : SLICES + 2], rest[SLICES + 2], rest[SLICES + 3]
    z0, core, lo, rank = where_ref[0], where_ref[1], where_ref[2], where_ref[3]
    sign = 1 - 2 * core

    slots = []
    for first, n in groups:
        begin = len(slots)
        slots += [None] + [(e, first <= e < first + n) for e in range(first - 1, first + n + 1)] + [None]
    for at, slot in enumerate(slots):
        if slot is None:
            for field in fields:
                field[at] = jnp.zeros(field.shape[1:], field.dtype)
    held = {at: slot for at, slot in enumerate(slots) if slot is not None}

    def half_of(e):
        return core if e % 2 == 0 else 1 - core

    def plane_block(e):
        return 2 * lax.rem(z0 + sign * (e // 2) + 2 * ZS, ZS) + half_of(e)

    for at, (e, _) in held.items():
        b, half = plane_block(e), half_of(e)
        index = jnp.where(half == lo, 0, 1)
        for ref, (z_at, mine) in zip(pieces, holders):
            if (z_at - e // 2) % ZS:
                continue
            side = core if mine else 1 - core
            tile = ref[index, 0 : HALF[0], :].astype(jnp.float32)
            t_re, t_im = cosine_sine(tile)
            for wv in range(2):
                rows = pl.ds(pl.multiple_of(side * HALF[0], 16), HALF[0])
                x_re, x_im = x_wave[b, wv, 0:1, :], x_wave[b, wv, 1:2, :]
                y_re, y_im = y_wave[wv, 0, rows, :], y_wave[wv, 1, rows, :]
                re, im = x_re * y_re - x_im * y_im, x_re * y_im + x_im * y_re
                rows = pl.ds(pl.multiple_of(wv * IN_ROWS[0] + side * HALF[0], 16), HALF[0])
                fields[0][at, rows, 0:LANES] = (re * t_re - im * t_im).astype(jnp.bfloat16)
                fields[0][at, rows, LANES:] = (re * t_im + im * t_re).astype(jnp.bfloat16)
            for s in range(1, SLICES):
                tile = ref[index, HALF_AT[s] : HALF_AT[s] + HALF[s], :].astype(jnp.float32)
                re, im = cosine_sine(tile)
                rows = pl.ds(pl.multiple_of(side * HALF[s], 16), HALF[s])
                trans[s - 1][at, rows, 0:LANES] = re.astype(jnp.bfloat16)
                trans[s - 1][at, rows, LANES:] = im.astype(jnp.bfloat16)

    for edge, low in ((0, True), (RANKS - 1, False)):

        @pl.when(rank == edge)
        def _(low=low):
            for s in range(1, SLICES):
                rows = slice(0, HALO[s]) if low else slice(HALO[s] + ROWS, IN_ROWS[s])
                for at in held:
                    trans[s - 1][at, rows, :] = jnp.zeros((HALO[s], 2 * LANES), jnp.bfloat16)

    for s in range(SLICES):
        rows_in, rows_out = IN_ROWS[s], IN_ROWS[s] - 2 * REACH
        here, there = fields[s % 2], fields[(s + 1) % 2]
        lane = lax.broadcasted_iota(jnp.int32, (2 * rows_in, 2 * LANES), 1)
        from_left = (lane & (LANES - 1)) >= LANES // 2
        active = {at: slot for at, slot in held.items() if s + 1 < SLICES or slot[1]}
        halves = []
        for at, (e, _) in active.items():
            b = plane_block(e)
            left = here[jnp.where(b == 0, 0, at - sign), 0 : 2 * rows_in, :]
            right = here[jnp.where(b == BLOCKS - 1, 0, at + sign), 0 : 2 * rows_in, :]
            edges = jnp.where(from_left, left, right)
            both = jnp.concatenate([here[at, 0 : 2 * rows_in, :], edges], axis=1)
            h = jnp.dot(both, weights[...], preferred_element_type=jnp.float32).astype(jnp.bfloat16)
            re = jnp.concatenate([h[:rows_in, :LANES], h[rows_in:, :LANES]], axis=1)
            im = jnp.concatenate([h[:rows_in, LANES:], h[rows_in:, LANES:]], axis=1)
            halves.append(jnp.concatenate([re, im], axis=0))
        number = 0
        for (at, (e, _)), h in zip(active.items(), halves):
            full = jnp.dot(rows_band[s][...], h, preferred_element_type=jnp.float32)
            for wv in range(2):
                re = full[:rows_out, wv * LANES : (wv + 1) * LANES]
                im = full[rows_out:, wv * LANES : (wv + 1) * LANES]
                if s + 1 < SLICES:
                    t_re = trans[s][at, :, :LANES].astype(jnp.float32)
                    t_im = trans[s][at, :, LANES:].astype(jnp.float32)
                    rows = slice(wv * rows_out, (wv + 1) * rows_out)
                    there[at, rows, 0:LANES] = (re * t_re - im * t_im).astype(jnp.bfloat16)
                    there[at, rows, LANES:] = (re * t_im + im * t_re).astype(jnp.bfloat16)
                else:
                    made[number, 0, wv] = re.astype(jnp.bfloat16)
                    made[number, 1, wv] = im.astype(jnp.bfloat16)
            if s + 1 == SLICES:
                number += 1

    copies = []
    for number, (e, _) in enumerate(slot for slot in held.values() if slot[1]):
        columns = pl.ds(pl.multiple_of(plane_block(e) * LANES, LANES), LANES)
        copies.append(pltpu.make_async_copy(made.at[number], out.at[:, :, :, columns], sems.at[number]))
        copies[-1].start()
    for copy in copies:
        copy.wait()


def blocks_of(groups, holders, where, pieces, constants, out):
    count = sum(n for _, n in groups)
    slots = count + 4 * len(groups)
    vmem = pl.BlockSpec(memory_space=pltpu.VMEM)
    operands = [*pieces, *constants]
    specs = [pl.BlockSpec(memory_space=pltpu.SMEM)] + [vmem] * len(operands)
    aliases = {}
    if out is not None:
        operands.append(out)
        specs.append(pl.BlockSpec(memory_space=pl.ANY))
        aliases = {len(specs) - 1: 0}
    work = slots * 10**9 // 2
    return pl.pallas_call(
        functools.partial(body, groups, holders, out is None),
        out_shape=jax.ShapeDtypeStruct((2, 2, ROWS, NX), jnp.bfloat16),
        in_specs=specs,
        out_specs=pl.BlockSpec(memory_space=pl.ANY),
        input_output_aliases=aliases,
        scratch_shapes=[pltpu.VMEM((slots, n, 2 * LANES), jnp.bfloat16) for n in IN_ROWS[1:]]
        + [pltpu.VMEM((slots, 2 * IN_ROWS[s], 2 * LANES), jnp.bfloat16) for s in range(2)]
        + [pltpu.VMEM((count, 2, 2, ROWS, LANES), jnp.bfloat16), pltpu.SemaphoreType.DMA((count,))],
        compiler_params=pltpu.CompilerParams(vmem_limit_bytes=40 * 2**20),
        cost_estimate=pl.CostEstimate(flops=work, bytes_accessed=2**20, transcendentals=0),
    )(where, *operands)


def per_device(potential, tilt_index):
    wave_at, rank = lax.axis_index("wave"), lax.axis_index("rows")
    z, lo, core = wave_at // 4, (wave_at // 2) % 2, wave_at % 2
    first = core == 0

    def by_core(mine, other):
        return jnp.concatenate([jnp.where(first, mine, other), jnp.where(first, other, mine)], axis=-1)

    pair = send(potential, to_pair)
    own = by_core(potential, send(potential, to_core))
    pair = by_core(pair, send(pair, to_core))
    rows = jnp.stack([own, pair])
    down = [rows[:, s, ROWS - HALO[s] :] for s in range(SLICES)]
    up = [rows[:, s, : HALO[s]] for s in range(SLICES)]
    halo = send(jnp.where(first, jnp.concatenate(down, axis=1), jnp.concatenate(up, axis=1)), to_rank)

    top, bottom = [], []
    for s in range(SLICES):
        piece = halo[:, sum(HALO[:s]) : sum(HALO[: s + 1])]
        top += [piece, rows[:, s, :CORE_ROWS]]
        bottom += [rows[:, s, CORE_ROWS:], piece]
    mine = jnp.where(first, jnp.concatenate(top, axis=1), jnp.concatenate(bottom, axis=1))
    other = send(mine, to_core)

    tilt_index, _ = lax.optimization_barrier((tilt_index, halo))
    y = rank * ROWS - HALO[0] + jnp.arange(IN_ROWS[0], dtype=jnp.int32)
    inside = ((y >= 0) & (y < NY)).astype(jnp.float32)
    turn_y = (tilt_index[:, 0:1] * y[None, :] % NY).astype(jnp.float32) * (2.0 * math.pi / NY)
    y_wave = jnp.stack([jnp.cos(turn_y) * inside, jnp.sin(turn_y) * inside], axis=1)
    y_wave = jnp.broadcast_to(y_wave[..., None], (*y_wave.shape, LANES))
    x = jnp.arange(NX, dtype=jnp.int32)
    turn_x = (tilt_index[:, 1:2] * x[None, :] % NX).astype(jnp.float32) * (2.0 * math.pi / NX)
    x_wave = jnp.stack([jnp.cos(turn_x), jnp.sin(turn_x)], axis=1)
    x_wave = x_wave.reshape(2, 2, BLOCKS, LANES).transpose(2, 0, 1, 3)
    constants = [jnp.asarray(column_weights(), jnp.bfloat16)]
    constants += [jnp.asarray(row_weights(s), jnp.bfloat16) for s in range(SLICES)]
    constants += [x_wave, y_wave]
    where = jnp.stack([z, core, lo, rank]).astype(jnp.int32)

    held = {(0, True): mine, (0, False): other}
    out = None
    for k, groups in CALLS:
        mine = send(mine, to_next)
        held[-k, True], held[k, False] = mine, send(mine, to_core)
        if k < ZS // 2:
            other = send(other, to_next)
            held[-k, False], held[k, True] = other, send(other, to_core)
        used = {(e // 2) % ZS for at, n in groups for e in range(at - 1, at + n + 1)}
        holders = tuple(key for key in held if key[0] % ZS in used)
        out = blocks_of(groups, holders, where, [held[key] for key in holders], constants, out)
    return out


def solution(mesh):
    return jax.shard_map(
        per_device,
        mesh=mesh,
        in_specs=(P(None, "rows", "wave"), P("wave", None)),
        out_specs=P(None, "wave", "rows", None),
        check_vma=False,
    )
```

```python
import functools
import math

import jax
import jax.numpy as jnp
import numpy as np
from jax import lax
from jax.experimental import pallas as pl
from jax.experimental.pallas import tpu as pltpu
from jax.sharding import PartitionSpec as P

NX = 2048
NY = 512
TAPS = 33
REACH = TAPS // 2
SLICES = 4
ROWS = 64
LANES = 128
BLOCKS = NX // LANES
ZS, WAVE, RANKS = 8, 32, 8
HALO = [REACH * (SLICES - s) for s in range(SLICES)]
IN_ROWS = [ROWS + 2 * h for h in HALO]
HALF = [n // 2 for n in IN_ROWS]
HALF_AT = [sum(HALF[:s]) for s in range(SLICES)]
HALF_ALL = sum(HALF)
BOTH = ("wave", "rows")
CORE_ROWS = ROWS // 2
HALO_ALL = sum(HALO)


def place(z, lo, core, rank):
    return ((z * 2 + lo) * 2 + core) * RANKS + rank


def send(value, target_of):
    pairs = []
    for z in range(ZS):
        for lo in range(2):
            for core in range(2):
                for rank in range(RANKS):
                    target = target_of(z, lo, core, rank)
                    if target is not None:
                        pairs.append((place(z, lo, core, rank), place(*target)))
    return lax.ppermute(value, BOTH, pairs)


def to_core(z, lo, core, rank):
    return z, lo, 1 - core, rank


def to_pair(z, lo, core, rank):
    return z, 1 - lo, core, rank


def to_rank(z, lo, core, rank):
    rank += 1 - 2 * core
    return (z, lo, core, rank) if 0 <= rank < RANKS else None


def to_next(z, lo, core, rank):
    return (z + 1 - 2 * core) % ZS, lo, core, rank


def taps():
    d = np.arange(TAPS, dtype=np.float32) - REACH
    angle = np.float32(math.pi) * d * d / TAPS
    scale = np.float32(1.0 / math.sqrt(TAPS))
    return np.cos(angle) * scale, np.sin(angle) * scale


def band(inside, outside, shift):
    at = np.arange(inside)[:, None] - np.arange(outside)[None, :] + shift
    valid = (at >= 0) & (at < TAPS)
    at = np.clip(at, 0, TAPS - 1)
    return tuple(np.where(valid, part[at], np.float32(0.0)) for part in taps())


def column_weights():
    def packed(re, im):
        return np.block([[re, im], [-im, re]])

    middle = band(LANES, LANES, REACH)
    left = band(LANES, LANES, REACH - LANES)
    right = band(LANES, LANES, REACH + LANES)
    return np.concatenate([packed(*middle), packed(left[0] + right[0], left[1] + right[1])])


def row_weights(s):
    re, im = (part.T for part in band(IN_ROWS[s], IN_ROWS[s] - 2 * REACH, 0))
    return np.block([[re, -im], [im, re]])


def polynomial(func, degree):
    w = 0.125 * (1.0 + np.cos(np.pi * (np.arange(64) + 0.5) / 64))
    fit = np.polynomial.chebyshev.Chebyshev.fit(w, func(3.0 * np.sqrt(w)), degree, domain=[0.0, 0.25])
    return [float(c) for c in fit.convert(kind=np.polynomial.Polynomial).coef]


EVEN = polynomial(np.cos, 4)
ODD = polynomial(lambda x: np.sin(x) / (x / 3.0), 4)


def horner(coefs, w):
    total = jnp.full_like(w, coefs[-1])
    for c in coefs[-2::-1]:
        total = total * w + c
    return total


def cosine_sine(tile):
    v = tile - 0.5
    w = v * v
    cos_v, sin_v = horner(EVEN, w), horner(ODD, w) * v
    c, s = math.cos(1.5), math.sin(1.5)
    return cos_v * c - sin_v * s, cos_v * s + sin_v * c


ROUNDS = (2, 3, 4)


def new_blocks(call, s):
    k = ROUNDS[call]
    if call == 0:
        return [(-2 * k + 1 + s, 2 * k - s)]
    p = ROUNDS[call - 1]
    if k < ZS // 2:
        return [(-2 * k + 1 + s, -2 * p + s), (2 * p - s + 1, 2 * k - s)]
    return [(2 * p - s + 1, BLOCKS - 2 * p + s)]


def kept_blocks(call, s):
    k = ROUNDS[call]
    return (-2 * k + s, -2 * k + s + 1, 2 * k - s, 2 * k + 1 - s)


def members(runs):
    return [e for low, high in runs for e in range(low, high + 1)]


def slots_of(call, s):
    return {e: at + 1 for at, e in enumerate(members([(low - 1, high + 1) for low, high in new_blocks(call, s)]))}


def trans_of(call, s):
    return {e: at for at, e in enumerate(members(new_blocks(call, s - 1)))}


def zs_of(call):
    wanted = set(slots_of(call, 0))
    for s in range(1, SLICES):
        wanted |= set(trans_of(call, s))
    return {(e // 2) % ZS for e in wanted}


def body(call, holders, where_ref, *refs):
    refs = list(refs)

    def take(n):
        taken = refs[:n]
        del refs[:n]
        return taken

    last = call == len(ROUNDS) - 1
    pieces = take(len(holders))
    (weights,), rows_band, (x_wave, y_wave) = take(1), take(SLICES), take(2)
    kept_in = take(SLICES - 1) if call else None
    if call:
        take(1)
    (out,) = take(1)
    kept_out = None if last else take(SLICES - 1)
    trans, fields, (made, sems) = take(SLICES - 1), take(SLICES), take(2)
    z0, core, lo, rank = where_ref[0], where_ref[1], where_ref[2], where_ref[3]
    sign = 1 - 2 * core
    slots = [slots_of(call, s) for s in range(SLICES)]

    def half_of(e):
        return core if e % 2 == 0 else 1 - core

    def plane_block(e):
        return 2 * lax.rem(z0 + sign * (e // 2) + 2 * ZS, ZS) + half_of(e)

    def parts_of(e):
        index = jnp.where(half_of(e) == lo, 0, 1)
        sides = set()
        for ref, (z_at, mine) in zip(pieces, holders):
            if (z_at - e // 2) % ZS == 0 and mine not in sides:
                sides.add(mine)
                yield ref, index, core if mine else 1 - core

    for s in range(SLICES):
        fields[s][0] = jnp.zeros(fields[s].shape[1:], fields[s].dtype)
        if call and s:
            for at, e in enumerate(kept_blocks(call - 1, s)):
                e = e if e in slots[s] else e + BLOCKS
                fields[s][slots[s][e]] = kept_in[s - 1][at]

    for e, at in slots[0].items():
        b = plane_block(e)
        for ref, index, side in parts_of(e):
            t_re, t_im = cosine_sine(ref[index, 0 : HALF[0], :].astype(jnp.float32))
            for wv in range(2):
                rows = pl.ds(pl.multiple_of(side * HALF[0], 16), HALF[0])
                x_re, x_im = x_wave[b, wv, 0:1, :], x_wave[b, wv, 1:2, :]
                y_re, y_im = y_wave[wv, 0, rows, :], y_wave[wv, 1, rows, :]
                re, im = x_re * y_re - x_im * y_im, x_re * y_im + x_im * y_re
                rows = pl.ds(pl.multiple_of(wv * IN_ROWS[0] + side * HALF[0], 16), HALF[0])
                fields[0][at, rows, 0:LANES] = (re * t_re - im * t_im).astype(jnp.bfloat16)
                fields[0][at, rows, LANES:] = (re * t_im + im * t_re).astype(jnp.bfloat16)
    for s in range(1, SLICES):
        for e, at in trans_of(call, s).items():
            for ref, index, side in parts_of(e):
                re, im = cosine_sine(ref[index, HALF_AT[s] : HALF_AT[s] + HALF[s], :].astype(jnp.float32))
                rows = pl.ds(pl.multiple_of(side * HALF[s], 16), HALF[s])
                trans[s - 1][at, rows, 0:LANES] = re.astype(jnp.bfloat16)
                trans[s - 1][at, rows, LANES:] = im.astype(jnp.bfloat16)

    for edge, low in ((0, True), (RANKS - 1, False)):

        @pl.when(rank == edge)
        def _(low=low):
            for s in range(1, SLICES):
                rows = slice(0, HALO[s]) if low else slice(HALO[s] + ROWS, IN_ROWS[s])
                for at in trans_of(call, s).values():
                    trans[s - 1][at, rows, :] = jnp.zeros((HALO[s], 2 * LANES), jnp.bfloat16)

    for s in range(SLICES):
        rows_in, rows_out = IN_ROWS[s], IN_ROWS[s] - 2 * REACH
        lane = lax.broadcasted_iota(jnp.int32, (2 * rows_in, 2 * LANES), 1)
        from_left = (lane & (LANES - 1)) >= LANES // 2
        blocks = members(new_blocks(call, s))
        halves = []
        for e in blocks:
            at, b = slots[s][e], plane_block(e)
            left = fields[s][jnp.where(b == 0, 0, at - sign)]
            right = fields[s][jnp.where(b == BLOCKS - 1, 0, at + sign)]
            both = jnp.concatenate([fields[s][at], jnp.where(from_left, left, right)], axis=1)
            h = jnp.dot(both, weights[...], preferred_element_type=jnp.float32).astype(jnp.bfloat16)
            re = jnp.concatenate([h[:rows_in, :LANES], h[rows_in:, :LANES]], axis=1)
            im = jnp.concatenate([h[:rows_in, LANES:], h[rows_in:, LANES:]], axis=1)
            halves.append(jnp.concatenate([re, im], axis=0))
        for number, (e, h) in enumerate(zip(blocks, halves)):
            full = jnp.dot(rows_band[s][...], h, preferred_element_type=jnp.float32)
            for wv in range(2):
                re = full[:rows_out, wv * LANES : (wv + 1) * LANES]
                im = full[rows_out:, wv * LANES : (wv + 1) * LANES]
                if s + 1 < SLICES:
                    t = trans[s].at[trans_of(call, s + 1)[e]]
                    t_re, t_im = t[:, :LANES].astype(jnp.float32), t[:, LANES:].astype(jnp.float32)
                    re, im = (re * t_re - im * t_im).astype(jnp.bfloat16), (re * t_im + im * t_re).astype(jnp.bfloat16)
                    rows = slice(wv * rows_out, (wv + 1) * rows_out)
                    targets = [fields[s + 1].at[slots[s + 1][e]]]
                    if not last:
                        kept = kept_blocks(call, s + 1)
                        targets += [kept_out[s].at[at] for at in range(4) if kept[at] == e]
                    for target in targets:
                        target[rows, 0:LANES] = re
                        target[rows, LANES:] = im
                else:
                    made[number, 0, wv] = re.astype(jnp.bfloat16)
                    made[number, 1, wv] = im.astype(jnp.bfloat16)
            if s + 1 == SLICES:
                columns = pl.ds(pl.multiple_of(plane_block(e) * LANES, LANES), LANES)
                pltpu.make_async_copy(made.at[number], out.at[:, :, :, columns], sems.at[number]).start()

    for number, e in enumerate(members(new_blocks(call, SLICES - 1))):
        columns = pl.ds(pl.multiple_of(plane_block(e) * LANES, LANES), LANES)
        pltpu.make_async_copy(made.at[number], out.at[:, :, :, columns], sems.at[number]).wait()


def propagate(call, holders, where, pieces, constants, carried):
    vmem, anywhere = pl.BlockSpec(memory_space=pltpu.VMEM), pl.BlockSpec(memory_space=pl.ANY)
    operands = [*pieces, *constants]
    specs = [pl.BlockSpec(memory_space=pltpu.SMEM)] + [vmem] * len(operands)
    aliases = {}
    if carried is not None:
        out, *kept = carried
        operands += [*kept, out]
        specs += [vmem] * len(kept) + [anywhere]
        aliases = {len(specs) - 1: 0}
    shapes = [jax.ShapeDtypeStruct((2, 2, ROWS, NX), jnp.bfloat16)]
    if call < len(ROUNDS) - 1:
        shapes += [jax.ShapeDtypeStruct((4, 2 * n, 2 * LANES), jnp.bfloat16) for n in IN_ROWS[1:]]
    made = len(members(new_blocks(call, SLICES - 1)))
    scratch = [pltpu.VMEM((len(trans_of(call, s)), IN_ROWS[s], 2 * LANES), jnp.bfloat16) for s in range(1, SLICES)]
    scratch += [pltpu.VMEM((len(slots_of(call, s)) + 1, 2 * IN_ROWS[s], 2 * LANES), jnp.bfloat16) for s in range(SLICES)]
    scratch += [pltpu.VMEM((made, 2, 2, ROWS, LANES), jnp.bfloat16), pltpu.SemaphoreType.DMA((made,))]
    return pl.pallas_call(
        functools.partial(body, call, holders),
        out_shape=shapes,
        in_specs=specs,
        out_specs=[anywhere] + [vmem] * (len(shapes) - 1),
        input_output_aliases=aliases,
        scratch_shapes=scratch,
        compiler_params=pltpu.CompilerParams(vmem_limit_bytes=40 * 2**20),
        cost_estimate=pl.CostEstimate(flops=3 * 10**9, bytes_accessed=2**20, transcendentals=0),
    )(where, *operands)


def per_device(potential, tilt_index):
    wave_at, rank = lax.axis_index("wave"), lax.axis_index("rows")
    z, lo, core = wave_at // 4, (wave_at // 2) % 2, wave_at % 2
    first = core == 0

    def by_core(mine, other):
        return jnp.concatenate([jnp.where(first, mine, other), jnp.where(first, other, mine)], axis=-1)

    pair = send(potential, to_pair)
    own = by_core(potential, send(potential, to_core))
    pair = by_core(pair, send(pair, to_core))
    rows = jnp.stack([own, pair])
    down = [rows[:, s, ROWS - HALO[s] :] for s in range(SLICES)]
    up = [rows[:, s, : HALO[s]] for s in range(SLICES)]
    halo = send(jnp.where(first, jnp.concatenate(down, axis=1), jnp.concatenate(up, axis=1)), to_rank)

    top, bottom = [], []
    for s in range(SLICES):
        piece = halo[:, sum(HALO[:s]) : sum(HALO[: s + 1])]
        top += [piece, rows[:, s, :CORE_ROWS]]
        bottom += [rows[:, s, CORE_ROWS:], piece]
    mine = jnp.where(first, jnp.concatenate(top, axis=1), jnp.concatenate(bottom, axis=1))
    other = send(mine, to_core)

    tilt_index, _ = lax.optimization_barrier((tilt_index, halo))
    y = rank * ROWS - HALO[0] + jnp.arange(IN_ROWS[0], dtype=jnp.int32)
    inside = ((y >= 0) & (y < NY)).astype(jnp.float32)
    turn_y = (tilt_index[:, 0:1] * y[None, :] % NY).astype(jnp.float32) * (2.0 * math.pi / NY)
    y_wave = jnp.stack([jnp.cos(turn_y) * inside, jnp.sin(turn_y) * inside], axis=1)
    y_wave = jnp.broadcast_to(y_wave[..., None], (*y_wave.shape, LANES))
    x = jnp.arange(NX, dtype=jnp.int32)
    turn_x = (tilt_index[:, 1:2] * x[None, :] % NX).astype(jnp.float32) * (2.0 * math.pi / NX)
    x_wave = jnp.stack([jnp.cos(turn_x), jnp.sin(turn_x)], axis=1)
    x_wave = x_wave.reshape(2, 2, BLOCKS, LANES).transpose(2, 0, 1, 3)
    constants = [jnp.asarray(column_weights(), jnp.bfloat16)]
    constants += [jnp.asarray(row_weights(s), jnp.bfloat16) for s in range(SLICES)]
    constants += [x_wave, y_wave]
    where = jnp.stack([z, core, lo, rank]).astype(jnp.int32)

    held = {(0, True): mine, (0, False): other}
    calls = []
    for k in range(1, ZS // 2 + 1):
        if k == ZS // 2:
            mine, _ = lax.optimization_barrier((mine, calls[0][1]))
        mine = send(mine, to_next)
        swap = mine
        if k == ZS // 2:
            swap, _ = lax.optimization_barrier((mine, calls[1][1]))
        held[-k, True], held[k, False] = mine, send(swap, to_core)
        if k < ZS // 2:
            other = send(other, to_next)
            held[-k, False], held[k, True] = other, send(other, to_core)
        if k in ROUNDS:
            call = ROUNDS.index(k)
            holders = tuple(key for key in held if key[0] % ZS in zs_of(call))
            pieces = [held[key] for key in holders]
            calls.append(propagate(call, holders, where, pieces, constants, calls[-1] if calls else None))
    return calls[-1][0]


def solution(mesh):
    return jax.shard_map(
        per_device,
        mesh=mesh,
        in_specs=(P(None, "rows", "wave"), P("wave", None)),
        out_specs=P(None, "wave", "rows", None),
        check_vma=False,
    )
```

```python
import functools
import math

import jax
import jax.numpy as jnp
import numpy as np
from jax import lax
from jax.experimental import pallas as pl
from jax.experimental.pallas import tpu as pltpu
from jax.sharding import PartitionSpec as P

NX = 2048
NY = 512
TAPS = 33
REACH = TAPS // 2
SLICES = 4
ROWS = 64
LANES = 128
BLOCKS = NX // LANES
ZS, WAVE, RANKS = 8, 32, 8
HALO = [REACH * (SLICES - s) for s in range(SLICES)]
IN_ROWS = [ROWS + 2 * h for h in HALO]
HALF = [n // 2 for n in IN_ROWS]
HALF_AT = [sum(HALF[:s]) for s in range(SLICES)]
HALF_ALL = sum(HALF)
BOTH = ("wave", "rows")
CORE_ROWS = ROWS // 2
HALO_ALL = sum(HALO)


def place(z, lo, core, rank):
    return ((z * 2 + lo) * 2 + core) * RANKS + rank


def send(value, target_of):
    pairs = []
    for z in range(ZS):
        for lo in range(2):
            for core in range(2):
                for rank in range(RANKS):
                    target = target_of(z, lo, core, rank)
                    if target is not None:
                        pairs.append((place(z, lo, core, rank), place(*target)))
    return lax.ppermute(value, BOTH, pairs)


def to_core(z, lo, core, rank):
    return z, lo, 1 - core, rank


def to_pair(z, lo, core, rank):
    return z, 1 - lo, core, rank


def to_rank(z, lo, core, rank):
    rank += 1 - 2 * core
    return (z, lo, core, rank) if 0 <= rank < RANKS else None


def to_next(z, lo, core, rank):
    return (z + 1 - 2 * core) % ZS, lo, core, rank


def taps():
    d = np.arange(TAPS, dtype=np.float32) - REACH
    angle = np.float32(math.pi) * d * d / TAPS
    scale = np.float32(1.0 / math.sqrt(TAPS))
    return np.cos(angle) * scale, np.sin(angle) * scale


def band(inside, outside, shift):
    at = np.arange(inside)[:, None] - np.arange(outside)[None, :] + shift
    valid = (at >= 0) & (at < TAPS)
    at = np.clip(at, 0, TAPS - 1)
    return tuple(np.where(valid, part[at], np.float32(0.0)) for part in taps())


def column_weights():
    def packed(re, im):
        return np.block([[re, im], [-im, re]])

    middle = band(LANES, LANES, REACH)
    left = band(LANES, LANES, REACH - LANES)
    right = band(LANES, LANES, REACH + LANES)
    return np.concatenate([packed(*middle), packed(left[0] + right[0], left[1] + right[1])])


def row_weights(s):
    re, im = (part.T for part in band(IN_ROWS[s], IN_ROWS[s] - 2 * REACH, 0))
    return np.block([[re, -im], [im, re]])


def polynomial(func, degree):
    w = 0.125 * (1.0 + np.cos(np.pi * (np.arange(64) + 0.5) / 64))
    fit = np.polynomial.chebyshev.Chebyshev.fit(w, func(3.0 * np.sqrt(w)), degree, domain=[0.0, 0.25])
    return [float(c) for c in fit.convert(kind=np.polynomial.Polynomial).coef]


EVEN = polynomial(np.cos, 4)
ODD = polynomial(lambda x: np.sin(x) / (x / 3.0), 4)


def horner(coefs, w):
    total = jnp.full_like(w, coefs[-1])
    for c in coefs[-2::-1]:
        total = total * w + c
    return total


def cosine_sine(tile):
    v = tile - 0.5
    w = v * v
    cos_v, sin_v = horner(EVEN, w), horner(ODD, w) * v
    c, s = math.cos(1.5), math.sin(1.5)
    return cos_v * c - sin_v * s, cos_v * s + sin_v * c


ROUNDS = (2, 3, 4)


def new_blocks(call, s):
    k = ROUNDS[call]
    if call == 0:
        return [(-2 * k + 1 + s, 2 * k - s)]
    p = ROUNDS[call - 1]
    if k < ZS // 2:
        return [(-2 * k + 1 + s, -2 * p + s), (2 * p - s + 1, 2 * k - s)]
    return [(2 * p - s + 1, BLOCKS - 2 * p + s)]


def kept_blocks(call, s):
    k = ROUNDS[call]
    return (-2 * k + s, -2 * k + s + 1, 2 * k - s, 2 * k + 1 - s)


def members(runs):
    return [e for low, high in runs for e in range(low, high + 1)]


def slots_of(call, s):
    return {e: at + 1 for at, e in enumerate(members([(low - 1, high + 1) for low, high in new_blocks(call, s)]))}


def trans_of(call, s):
    return {e: at for at, e in enumerate(members(new_blocks(call, s - 1)))}


def zs_of(call):
    wanted = set(slots_of(call, 0))
    for s in range(1, SLICES):
        wanted |= set(trans_of(call, s))
    return {(e // 2) % ZS for e in wanted}


def body(call, holders, where_ref, *refs):
    refs = list(refs)

    def take(n):
        taken = refs[:n]
        del refs[:n]
        return taken

    last = call == len(ROUNDS) - 1
    pieces = take(len(holders))
    (weights,), rows_band, (x_wave, y_wave) = take(1), take(SLICES), take(2)
    kept_in = take(SLICES - 1) if call else None
    done = take(call) if last else []
    (out,) = take(1) if last else (None,)
    kept_out = None if last else take(SLICES - 1)
    made = None if last else refs.pop(0)
    trans, fields = take(SLICES - 1), take(SLICES)
    if last:
        made, sems = take(2)
    z0, core, lo, rank = where_ref[0], where_ref[1], where_ref[2], where_ref[3]
    sign = 1 - 2 * core
    slots = [slots_of(call, s) for s in range(SLICES)]

    def half_of(e):
        return core if e % 2 == 0 else 1 - core

    def plane_block(e):
        return 2 * lax.rem(z0 + sign * (e // 2) + 2 * ZS, ZS) + half_of(e)

    def parts_of(e):
        index = jnp.where(half_of(e) == lo, 0, 1)
        sides = set()
        for ref, entries in zip(pieces, holders):
            for number, (z_at, mine) in enumerate(entries):
                if (z_at - e // 2) % ZS == 0 and mine not in sides:
                    sides.add(mine)
                    yield ref, 2 * number + index, core if mine else 1 - core

    copies = []

    def write(block, e):
        columns = pl.ds(pl.multiple_of(plane_block(e) * LANES, LANES), LANES)
        copies.append(pltpu.make_async_copy(block, out.at[:, :, :, columns], sems.at[len(copies)]))
        copies[-1].start()

    for earlier, blocks in enumerate(done):
        for number, e in enumerate(members(new_blocks(earlier, SLICES - 1))):
            write(blocks.at[number], e)

    for s in range(SLICES):
        fields[s][0] = jnp.zeros(fields[s].shape[1:], fields[s].dtype)
        if call and s:
            for at, e in enumerate(kept_blocks(call - 1, s)):
                e = e if e in slots[s] else e + BLOCKS
                fields[s][slots[s][e]] = kept_in[s - 1][at]

    for e, at in slots[0].items():
        b = plane_block(e)
        for ref, index, side in parts_of(e):
            t_re, t_im = cosine_sine(ref[index, 0 : HALF[0], :].astype(jnp.float32))
            for wv in range(2):
                rows = pl.ds(pl.multiple_of(side * HALF[0], 16), HALF[0])
                x_re, x_im = x_wave[b, wv, 0:1, :], x_wave[b, wv, 1:2, :]
                y_re, y_im = y_wave[wv, 0, rows, :], y_wave[wv, 1, rows, :]
                re, im = x_re * y_re - x_im * y_im, x_re * y_im + x_im * y_re
                rows = pl.ds(pl.multiple_of(wv * IN_ROWS[0] + side * HALF[0], 16), HALF[0])
                fields[0][at, rows, 0:LANES] = (re * t_re - im * t_im).astype(jnp.bfloat16)
                fields[0][at, rows, LANES:] = (re * t_im + im * t_re).astype(jnp.bfloat16)
    for s in range(1, SLICES):
        for e, at in trans_of(call, s).items():
            for ref, index, side in parts_of(e):
                re, im = cosine_sine(ref[index, HALF_AT[s] : HALF_AT[s] + HALF[s], :].astype(jnp.float32))
                rows = pl.ds(pl.multiple_of(side * HALF[s], 16), HALF[s])
                trans[s - 1][at, rows, 0:LANES] = re.astype(jnp.bfloat16)
                trans[s - 1][at, rows, LANES:] = im.astype(jnp.bfloat16)

    for edge, low in ((0, True), (RANKS - 1, False)):

        @pl.when(rank == edge)
        def _(low=low):
            for s in range(1, SLICES):
                rows = slice(0, HALO[s]) if low else slice(HALO[s] + ROWS, IN_ROWS[s])
                for at in trans_of(call, s).values():
                    trans[s - 1][at, rows, :] = jnp.zeros((HALO[s], 2 * LANES), jnp.bfloat16)

    for s in range(SLICES):
        rows_in, rows_out = IN_ROWS[s], IN_ROWS[s] - 2 * REACH
        lane = lax.broadcasted_iota(jnp.int32, (2 * rows_in, 2 * LANES), 1)
        from_left = (lane & (LANES - 1)) >= LANES // 2
        blocks = members(new_blocks(call, s))
        halves = []
        for e in blocks:
            at, b = slots[s][e], plane_block(e)
            left = fields[s][jnp.where(b == 0, 0, at - sign)]
            right = fields[s][jnp.where(b == BLOCKS - 1, 0, at + sign)]
            both = jnp.concatenate([fields[s][at], jnp.where(from_left, left, right)], axis=1)
            h = jnp.dot(both, weights[...], preferred_element_type=jnp.float32).astype(jnp.bfloat16)
            re = jnp.concatenate([h[:rows_in, :LANES], h[rows_in:, :LANES]], axis=1)
            im = jnp.concatenate([h[:rows_in, LANES:], h[rows_in:, LANES:]], axis=1)
            halves.append(jnp.concatenate([re, im], axis=0))
        for number, (e, h) in enumerate(zip(blocks, halves)):
            full = jnp.dot(rows_band[s][...], h, preferred_element_type=jnp.float32)
            for wv in range(2):
                re = full[:rows_out, wv * LANES : (wv + 1) * LANES]
                im = full[rows_out:, wv * LANES : (wv + 1) * LANES]
                if s + 1 < SLICES:
                    t = trans[s].at[trans_of(call, s + 1)[e]]
                    t_re, t_im = t[:, :LANES].astype(jnp.float32), t[:, LANES:].astype(jnp.float32)
                    re, im = (re * t_re - im * t_im).astype(jnp.bfloat16), (re * t_im + im * t_re).astype(jnp.bfloat16)
                    rows = slice(wv * rows_out, (wv + 1) * rows_out)
                    targets = [fields[s + 1].at[slots[s + 1][e]]]
                    if not last:
                        kept = kept_blocks(call, s + 1)
                        targets += [kept_out[s].at[at] for at in range(4) if kept[at] == e]
                    for target in targets:
                        target[rows, 0:LANES] = re
                        target[rows, LANES:] = im
                else:
                    made[number, 0, wv] = re.astype(jnp.bfloat16)
                    made[number, 1, wv] = im.astype(jnp.bfloat16)
            if last and s + 1 == SLICES:
                write(made.at[number], e)

    for copy in copies:
        copy.wait()


def propagate(call, holders, where, pieces, constants, kept, done):
    last = call == len(ROUNDS) - 1
    vmem, anywhere = pl.BlockSpec(memory_space=pltpu.VMEM), pl.BlockSpec(memory_space=pl.ANY)
    operands = [*pieces, *constants, *kept, *(done if last else ())]
    made = len(members(new_blocks(call, SLICES - 1)))
    scratch = [pltpu.VMEM((len(trans_of(call, s)), IN_ROWS[s], 2 * LANES), jnp.bfloat16) for s in range(1, SLICES)]
    scratch += [pltpu.VMEM((len(slots_of(call, s)) + 1, 2 * IN_ROWS[s], 2 * LANES), jnp.bfloat16) for s in range(SLICES)]
    if last:
        shapes = [jax.ShapeDtypeStruct((2, 2, ROWS, NX), jnp.bfloat16)]
        scratch += [pltpu.VMEM((made, 2, 2, ROWS, LANES), jnp.bfloat16), pltpu.SemaphoreType.DMA((BLOCKS,))]
    else:
        shapes = [jax.ShapeDtypeStruct((4, 2 * n, 2 * LANES), jnp.bfloat16) for n in IN_ROWS[1:]]
        shapes += [jax.ShapeDtypeStruct((made, 2, 2, ROWS, LANES), jnp.bfloat16)]
    return pl.pallas_call(
        functools.partial(body, call, holders),
        out_shape=shapes,
        in_specs=[pl.BlockSpec(memory_space=pltpu.SMEM)] + [vmem] * len(operands),
        out_specs=[anywhere if last else vmem] * len(shapes),
        scratch_shapes=scratch,
        compiler_params=pltpu.CompilerParams(vmem_limit_bytes=40 * 2**20),
        cost_estimate=pl.CostEstimate(flops=7 * 10**9, bytes_accessed=2**20, transcendentals=0),
    )(where, *operands)


def per_device(potential, tilt_index):
    wave_at, rank = lax.axis_index("wave"), lax.axis_index("rows")
    z, lo, core = wave_at // 4, (wave_at // 2) % 2, wave_at % 2
    first = core == 0

    def by_core(mine, other):
        return jnp.concatenate([jnp.where(first, mine, other), jnp.where(first, other, mine)], axis=-1)

    pair = send(potential, to_pair)
    own = by_core(potential, send(potential, to_core))
    pair = by_core(pair, send(pair, to_core))
    rows = jnp.stack([own, pair])
    down = [rows[:, s, ROWS - HALO[s] :] for s in range(SLICES)]
    up = [rows[:, s, : HALO[s]] for s in range(SLICES)]
    halo = send(jnp.where(first, jnp.concatenate(down, axis=1), jnp.concatenate(up, axis=1)), to_rank)

    top, bottom = [], []
    for s in range(SLICES):
        piece = halo[:, sum(HALO[:s]) : sum(HALO[: s + 1])]
        top += [piece, rows[:, s, :CORE_ROWS]]
        bottom += [rows[:, s, CORE_ROWS:], piece]
    mine = jnp.where(first, jnp.concatenate(top, axis=1), jnp.concatenate(bottom, axis=1))
    other = send(mine, to_core)

    tilt_index, _ = lax.optimization_barrier((tilt_index, halo))
    y = rank * ROWS - HALO[0] + jnp.arange(IN_ROWS[0], dtype=jnp.int32)
    inside = ((y >= 0) & (y < NY)).astype(jnp.float32)
    turn_y = (tilt_index[:, 0:1] * y[None, :] % NY).astype(jnp.float32) * (2.0 * math.pi / NY)
    y_wave = jnp.stack([jnp.cos(turn_y) * inside, jnp.sin(turn_y) * inside], axis=1)
    y_wave = jnp.broadcast_to(y_wave[..., None], (*y_wave.shape, LANES))
    x = jnp.arange(NX, dtype=jnp.int32)
    turn_x = (tilt_index[:, 1:2] * x[None, :] % NX).astype(jnp.float32) * (2.0 * math.pi / NX)
    x_wave = jnp.stack([jnp.cos(turn_x), jnp.sin(turn_x)], axis=1)
    x_wave = x_wave.reshape(2, 2, BLOCKS, LANES).transpose(2, 0, 1, 3)
    constants = [jnp.asarray(column_weights(), jnp.bfloat16)]
    constants += [jnp.asarray(row_weights(s), jnp.bfloat16) for s in range(SLICES)]
    constants += [x_wave, y_wave]
    where = jnp.stack([z, core, lo, rank]).astype(jnp.int32)

    held = {((0, True),): mine, ((0, False),): other}
    calls = []
    for k in range(1, ZS // 2 + 1):
        mine, other = send(mine, to_next), send(other, to_next)
        if k == ROUNDS[1]:
            mine, other, _ = lax.optimization_barrier((mine, other, calls[0][0]))
        held[((-k, True),)], held[((-k, False),)] = mine, other
        if k < ZS // 2:
            held[(k, False), (k, True)] = send(jnp.concatenate([mine, other], axis=0), to_core)
        if k in ROUNDS:
            call = ROUNDS.index(k)
            holders = tuple(key for key in held if key[0][0] % ZS in zs_of(call))
            pieces = [held[key] for key in holders]
            if k == ZS // 2:
                pieces[-1], _ = lax.optimization_barrier((pieces[-1], calls[1][0]))
            kept = calls[-1][:-1] if calls else []
            calls.append(propagate(call, holders, where, pieces, constants, kept, [made[-1] for made in calls]))
    return calls[-1][0]


def solution(mesh):
    return jax.shard_map(
        per_device,
        mesh=mesh,
        in_specs=(P(None, "rows", "wave"), P("wave", None)),
        out_specs=P(None, "wave", "rows", None),
        check_vma=False,
    )
```

```python
import functools
import math

import jax
import jax.numpy as jnp
import numpy as np
from jax import lax
from jax.experimental import pallas as pl
from jax.experimental.pallas import tpu as pltpu
from jax.sharding import PartitionSpec as P

NX = 2048
NY = 512
TAPS = 33
REACH = TAPS // 2
SLICES = 4
ROWS = 64
LANES = 128
BLOCKS = NX // LANES
ZS, WAVE, RANKS = 8, 32, 8
HALO = [REACH * (SLICES - s) for s in range(SLICES)]
IN_ROWS = [ROWS + 2 * h for h in HALO]
HALF = [n // 2 for n in IN_ROWS]
HALF_AT = [sum(HALF[:s]) for s in range(SLICES)]
HALF_ALL = sum(HALF)
BOTH = ("wave", "rows")
CORE_ROWS = ROWS // 2
HALO_ALL = sum(HALO)


def place(z, lo, core, rank):
    return ((z * 2 + lo) * 2 + core) * RANKS + rank


def send(value, target_of):
    pairs = []
    for z in range(ZS):
        for lo in range(2):
            for core in range(2):
                for rank in range(RANKS):
                    target = target_of(z, lo, core, rank)
                    if target is not None:
                        pairs.append((place(z, lo, core, rank), place(*target)))
    return lax.ppermute(value, BOTH, pairs)


def to_core(z, lo, core, rank):
    return z, lo, 1 - core, rank


def to_pair(z, lo, core, rank):
    return z, 1 - lo, core, rank


def to_rank(z, lo, core, rank):
    rank += 1 - 2 * core
    return (z, lo, core, rank) if 0 <= rank < RANKS else None


def to_next(z, lo, core, rank):
    return (z + 1 - 2 * core) % ZS, lo, core, rank


def taps():
    d = np.arange(TAPS, dtype=np.float32) - REACH
    angle = np.float32(math.pi) * d * d / TAPS
    scale = np.float32(1.0 / math.sqrt(TAPS))
    return np.cos(angle) * scale, np.sin(angle) * scale


def band(inside, outside, shift):
    at = np.arange(inside)[:, None] - np.arange(outside)[None, :] + shift
    valid = (at >= 0) & (at < TAPS)
    at = np.clip(at, 0, TAPS - 1)
    return tuple(np.where(valid, part[at], np.float32(0.0)) for part in taps())


def column_weights():
    def packed(re, im):
        return np.block([[re, im], [-im, re]])

    middle = band(LANES, LANES, REACH)
    left = band(LANES, LANES, REACH - LANES)
    right = band(LANES, LANES, REACH + LANES)
    return np.concatenate([packed(*middle), packed(left[0] + right[0], left[1] + right[1])])


def row_weights(s):
    re, im = (part.T for part in band(IN_ROWS[s], IN_ROWS[s] - 2 * REACH, 0))
    return np.block([[re, -im], [im, re]])


def polynomial(func, degree):
    w = 0.125 * (1.0 + np.cos(np.pi * (np.arange(64) + 0.5) / 64))
    fit = np.polynomial.chebyshev.Chebyshev.fit(w, func(3.0 * np.sqrt(w)), degree, domain=[0.0, 0.25])
    return [float(c) for c in fit.convert(kind=np.polynomial.Polynomial).coef]


EVEN = polynomial(np.cos, 4)
ODD = polynomial(lambda x: np.sin(x) / (x / 3.0), 4)


def horner(coefs, w):
    total = jnp.full_like(w, coefs[-1])
    for c in coefs[-2::-1]:
        total = total * w + c
    return total


def cosine_sine(tile):
    v = tile - 0.5
    w = v * v
    cos_v, sin_v = horner(EVEN, w), horner(ODD, w) * v
    c, s = math.cos(1.5), math.sin(1.5)
    return cos_v * c - sin_v * s, cos_v * s + sin_v * c


ROUNDS = (1, 2, 3, 4)


def propagated(k, s):
    return -2 * k + 1 + s, 2 * k - s


def new_blocks(call, s):
    low, high = propagated(ROUNDS[call], s)
    if call:
        low_before, high_before = propagated(ROUNDS[call - 1], s)
        if ROUNDS[call] == ZS // 2:
            return [(high_before + 1, BLOCKS + low_before - 1)]
        if low_before <= high_before:
            return [(low, low_before - 1), (high_before + 1, high)]
    return [(low, high)] if low <= high else []


def kept_blocks(call, s):
    k = ROUNDS[call]
    low, high = -2 * k + s, 2 * k + 1 - s
    return (low, low + 1, high - 1, high) if low <= high else ()


def members(runs):
    return [e for low, high in runs for e in range(low, high + 1)]


def slots_of(call, s):
    return {e: at + 1 for at, e in enumerate(members([(low - 1, high + 1) for low, high in new_blocks(call, s)]))}


def handed_on(call, s):
    kept = {e % BLOCKS: at for at, e in enumerate(kept_blocks(call - 1, s))} if call else {}
    return {e: (slot, kept[e % BLOCKS]) for e, slot in slots_of(call, s).items() if e % BLOCKS in kept}


def fresh_of(call):
    return {e: slot for e, slot in slots_of(call, 0).items() if e not in handed_on(call, 0)}


def trans_of(call, s):
    return {e: at for at, e in enumerate(members(new_blocks(call, s - 1)))}


def zs_of(call):
    wanted = set(fresh_of(call))
    for s in range(1, SLICES):
        wanted |= set(trans_of(call, s))
    return {(e // 2) % ZS for e in wanted}


def body(call, holders, where_ref, *refs):
    refs = list(refs)

    def take(n):
        taken = refs[:n]
        del refs[:n]
        return taken

    last = call == len(ROUNDS) - 1
    pieces = take(len(holders))
    (weights,), rows_band, (x_wave, y_wave) = take(1), take(SLICES), take(2)
    kept_in = take(SLICES) if call else None
    earlier_calls = [c for c in range(call) if new_blocks(c, SLICES - 1)] if last else []
    done = take(len(earlier_calls))
    (out,) = take(1) if last else (None,)
    kept_out = None if last else take(SLICES)
    made = refs.pop(0) if not last and new_blocks(call, SLICES - 1) else None
    trans, fields = take(SLICES - 1), take(SLICES)
    if last:
        made, sems = take(2)
    z0, core, lo, rank = where_ref[0], where_ref[1], where_ref[2], where_ref[3]
    sign = 1 - 2 * core
    slots = [slots_of(call, s) for s in range(SLICES)]

    def half_of(e):
        return core if e % 2 == 0 else 1 - core

    def plane_block(e):
        return 2 * lax.rem(z0 + sign * (e // 2) + 2 * ZS, ZS) + half_of(e)

    def parts_of(e):
        index = jnp.where(half_of(e) == lo, 0, 1)
        sides = set()
        for ref, entries in zip(pieces, holders):
            for number, (z_at, mine) in enumerate(entries):
                if (z_at - e // 2) % ZS == 0 and mine not in sides:
                    sides.add(mine)
                    yield ref, 2 * number + index, core if mine else 1 - core

    copies = []

    def write(block, e):
        columns = pl.ds(pl.multiple_of(plane_block(e) * LANES, LANES), LANES)
        copies.append(pltpu.make_async_copy(block, out.at[:, :, :, columns], sems.at[len(copies)]))
        copies[-1].start()

    for earlier, blocks in zip(earlier_calls, done):
        for number, e in enumerate(members(new_blocks(earlier, SLICES - 1))):
            write(blocks.at[number], e)

    for s in range(SLICES):
        fields[s][0] = jnp.zeros(fields[s].shape[1:], fields[s].dtype)
        for slot, at in handed_on(call, s).values():
            fields[s][slot] = kept_in[s][at]

    for e, at in fresh_of(call).items():
        kept = [] if last else [kept_out[0].at[k] for k, kept_e in enumerate(kept_blocks(call, 0)) if kept_e == e]
        b = plane_block(e)
        for ref, index, side in parts_of(e):
            t_re, t_im = cosine_sine(ref[index, 0 : HALF[0], :].astype(jnp.float32))
            for wv in range(2):
                rows = pl.ds(pl.multiple_of(side * HALF[0], 16), HALF[0])
                x_re, x_im = x_wave[b, wv, 0:1, :], x_wave[b, wv, 1:2, :]
                y_re, y_im = y_wave[wv, 0, rows, :], y_wave[wv, 1, rows, :]
                re, im = x_re * y_re - x_im * y_im, x_re * y_im + x_im * y_re
                rows = pl.ds(pl.multiple_of(wv * IN_ROWS[0] + side * HALF[0], 16), HALF[0])
                for target in (fields[0].at[at], *kept):
                    target[rows, 0:LANES] = (re * t_re - im * t_im).astype(jnp.bfloat16)
                    target[rows, LANES:] = (re * t_im + im * t_re).astype(jnp.bfloat16)
    for s in range(1, SLICES):
        for e, at in trans_of(call, s).items():
            for ref, index, side in parts_of(e):
                re, im = cosine_sine(ref[index, HALF_AT[s] : HALF_AT[s] + HALF[s], :].astype(jnp.float32))
                rows = pl.ds(pl.multiple_of(side * HALF[s], 16), HALF[s])
                trans[s - 1][at, rows, 0:LANES] = re.astype(jnp.bfloat16)
                trans[s - 1][at, rows, LANES:] = im.astype(jnp.bfloat16)

    for s in range(SLICES):
        rows_in, rows_out = IN_ROWS[s], IN_ROWS[s] - 2 * REACH
        lane = lax.broadcasted_iota(jnp.int32, (2 * rows_in, 2 * LANES), 1)
        from_left = (lane & (LANES - 1)) >= LANES // 2
        blocks = members(new_blocks(call, s))
        halves = []
        for e in blocks:
            at, b = slots[s][e], plane_block(e)
            left = fields[s][jnp.where(b == 0, 0, at - sign)]
            right = fields[s][jnp.where(b == BLOCKS - 1, 0, at + sign)]
            both = jnp.concatenate([fields[s][at], jnp.where(from_left, left, right)], axis=1)
            h = jnp.dot(both, weights[...], preferred_element_type=jnp.float32).astype(jnp.bfloat16)
            re = jnp.concatenate([h[:rows_in, :LANES], h[rows_in:, :LANES]], axis=1)
            im = jnp.concatenate([h[:rows_in, LANES:], h[rows_in:, LANES:]], axis=1)
            halves.append(jnp.concatenate([re, im], axis=0))
        for number, (e, h) in enumerate(zip(blocks, halves)):
            full = jnp.dot(rows_band[s][...], h, preferred_element_type=jnp.float32)
            for wv in range(2):
                re = full[:rows_out, wv * LANES : (wv + 1) * LANES]
                im = full[rows_out:, wv * LANES : (wv + 1) * LANES]
                if s + 1 < SLICES:
                    t = trans[s].at[trans_of(call, s + 1)[e]]
                    t_re, t_im = t[:, :LANES].astype(jnp.float32), t[:, LANES:].astype(jnp.float32)
                    re, im = (re * t_re - im * t_im).astype(jnp.bfloat16), (re * t_im + im * t_re).astype(jnp.bfloat16)
                    rows = slice(wv * rows_out, (wv + 1) * rows_out)
                    targets = [fields[s + 1].at[slots[s + 1][e]]] if e in slots[s + 1] else []
                    if not last:
                        kept = kept_blocks(call, s + 1)
                        targets += [kept_out[s + 1].at[at] for at, kept_e in enumerate(kept) if kept_e == e]
                    for target in targets:
                        target[rows, 0:LANES] = re
                        target[rows, LANES:] = im
                else:
                    made[number, 0, wv] = re.astype(jnp.bfloat16)
                    made[number, 1, wv] = im.astype(jnp.bfloat16)
            if last and s + 1 == SLICES:
                write(made.at[number], e)

    for copy in copies:
        copy.wait()


def propagate(call, holders, where, pieces, constants, kept, done):
    last = call == len(ROUNDS) - 1
    vmem, anywhere = pl.BlockSpec(memory_space=pltpu.VMEM), pl.BlockSpec(memory_space=pl.ANY)
    operands = [*pieces, *constants, *kept, *(done if last else ())]
    made = len(members(new_blocks(call, SLICES - 1)))
    scratch = [pltpu.VMEM((max(1, len(trans_of(call, s))), IN_ROWS[s], 2 * LANES), jnp.bfloat16) for s in range(1, SLICES)]
    scratch += [pltpu.VMEM((len(slots_of(call, s)) + 1, 2 * IN_ROWS[s], 2 * LANES), jnp.bfloat16) for s in range(SLICES)]
    if last:
        shapes = [jax.ShapeDtypeStruct((2, 2, ROWS, NX), jnp.bfloat16)]
        scratch += [pltpu.VMEM((made, 2, 2, ROWS, LANES), jnp.bfloat16), pltpu.SemaphoreType.DMA((BLOCKS,))]
    else:
        shapes = [jax.ShapeDtypeStruct((4, 2 * n, 2 * LANES), jnp.bfloat16) for n in IN_ROWS]
        if made:
            shapes += [jax.ShapeDtypeStruct((made, 2, 2, ROWS, LANES), jnp.bfloat16)]
    return pl.pallas_call(
        functools.partial(body, call, holders),
        out_shape=shapes,
        in_specs=[pl.BlockSpec(memory_space=pltpu.SMEM)] + [vmem] * len(operands),
        out_specs=[anywhere if last else vmem] * len(shapes),
        scratch_shapes=scratch,
        compiler_params=pltpu.CompilerParams(vmem_limit_bytes=40 * 2**20),
        cost_estimate=pl.CostEstimate(flops=(7 if call else 4) * 10**9, bytes_accessed=2**20, transcendentals=0),
    )(where, *operands)


def per_device(potential, tilt_index):
    wave_at, rank = lax.axis_index("wave"), lax.axis_index("rows")
    z, lo, core = wave_at // 4, (wave_at // 2) % 2, wave_at % 2
    first = core == 0

    def by_core(mine, other):
        return jnp.concatenate([jnp.where(first, mine, other), jnp.where(first, other, mine)], axis=-1)

    pair = send(potential, to_pair)
    own = by_core(potential, send(potential, to_core))
    pair = by_core(pair, send(pair, to_core))
    rows = jnp.stack([own, pair])
    down = [rows[:, s, ROWS - HALO[s] :] for s in range(SLICES)]
    up = [rows[:, s, : HALO[s]] for s in range(SLICES)]
    halo = send(jnp.where(first, jnp.concatenate(down, axis=1), jnp.concatenate(up, axis=1)), to_rank)

    top, bottom = [], []
    for s in range(SLICES):
        piece = halo[:, sum(HALO[:s]) : sum(HALO[: s + 1])]
        top += [piece, rows[:, s, :CORE_ROWS]]
        bottom += [rows[:, s, CORE_ROWS:], piece]
    mine = jnp.where(first, jnp.concatenate(top, axis=1), jnp.concatenate(bottom, axis=1))
    other = send(mine, to_core)

    tilt_index, _ = lax.optimization_barrier((tilt_index, halo))
    y = rank * ROWS - HALO[0] + jnp.arange(IN_ROWS[0], dtype=jnp.int32)
    inside = ((y >= 0) & (y < NY)).astype(jnp.float32)
    turn_y = (tilt_index[:, 0:1] * y[None, :] % NY).astype(jnp.float32) * (2.0 * math.pi / NY)
    y_wave = jnp.stack([jnp.cos(turn_y) * inside, jnp.sin(turn_y) * inside], axis=1)
    y_wave = jnp.broadcast_to(y_wave[..., None], (*y_wave.shape, LANES))
    x = jnp.arange(NX, dtype=jnp.int32)
    turn_x = (tilt_index[:, 1:2] * x[None, :] % NX).astype(jnp.float32) * (2.0 * math.pi / NX)
    x_wave = jnp.stack([jnp.cos(turn_x), jnp.sin(turn_x)], axis=1)
    x_wave = x_wave.reshape(2, 2, BLOCKS, LANES).transpose(2, 0, 1, 3)
    constants = [jnp.asarray(column_weights(), jnp.bfloat16)]
    for s in range(SLICES):
        y = rank * ROWS - HALO[s] + REACH + jnp.arange(IN_ROWS[s] - 2 * REACH, dtype=jnp.int32)
        keep = jnp.tile((y >= 0) & (y < NY), 2)[:, None]
        constants.append(jnp.where(keep, jnp.asarray(row_weights(s), jnp.bfloat16), 0))
    constants += [x_wave, y_wave]
    where = jnp.stack([z, core, lo, rank]).astype(jnp.int32)

    held = {((0, True),): mine, ((0, False),): other}
    calls = []
    for k in range(1, ZS // 2 + 1):
        mine, other = send(mine, to_next), send(other, to_next)
        if calls and k < ZS // 2:
            mine, other, _ = lax.optimization_barrier((mine, other, calls[-1][0]))
        held[((-k, True),)], held[((-k, False),)] = mine, other
        if k < ZS // 2:
            held[(k, False), (k, True)] = send(jnp.concatenate([mine, other], axis=0), to_core)
        if k in ROUNDS:
            call = ROUNDS.index(k)
            holders = tuple(key for key in held if key[0][0] % ZS in zs_of(call))
            pieces = [held[key] for key in holders]
            if k == ZS // 2:
                pieces[-1], _ = lax.optimization_barrier((pieces[-1], calls[-1][0]))
            kept = calls[-1][:SLICES] if calls else []
            done = [made[SLICES] for made in calls if len(made) > SLICES]
            calls.append(propagate(call, holders, where, pieces, constants, kept, done))
    return calls[-1][0]


def solution(mesh):
    return jax.shard_map(
        per_device,
        mesh=mesh,
        in_specs=(P(None, "rows", "wave"), P("wave", None)),
        out_specs=P(None, "wave", "rows", None),
        check_vma=False,
    )
```

```python
import functools
import math

import jax
import jax.numpy as jnp
import numpy as np
from jax import lax
from jax.experimental import pallas as pl
from jax.experimental.pallas import tpu as pltpu
from jax.sharding import PartitionSpec as P

NX = 2048
NY = 512
TAPS = 33
REACH = TAPS // 2
SLICES = 4
ROWS = 64
LANES = 128
BLOCKS = NX // LANES
ZS, WAVE, RANKS = 8, 32, 8
HALO = [REACH * (SLICES - s) for s in range(SLICES)]
IN_ROWS = [ROWS + 2 * h for h in HALO]
HALF = [n // 2 for n in IN_ROWS]
HALF_AT = [sum(HALF[:s]) for s in range(SLICES)]
HALF_ALL = sum(HALF)
BOTH = ("wave", "rows")
CORE_ROWS = ROWS // 2
HALO_ALL = sum(HALO)


def place(z, lo, core, rank):
    return ((z * 2 + lo) * 2 + core) * RANKS + rank


def send(value, target_of):
    pairs = []
    for z in range(ZS):
        for lo in range(2):
            for core in range(2):
                for rank in range(RANKS):
                    target = target_of(z, lo, core, rank)
                    if target is not None:
                        pairs.append((place(z, lo, core, rank), place(*target)))
    return lax.ppermute(value, BOTH, pairs)


def to_core(z, lo, core, rank):
    return z, lo, 1 - core, rank


def to_pair(z, lo, core, rank):
    return z, 1 - lo, core, rank


def to_rank(z, lo, core, rank):
    rank += 1 - 2 * core
    return (z, lo, core, rank) if 0 <= rank < RANKS else None


def to_next(z, lo, core, rank):
    return (z + 1 - 2 * core) % ZS, lo, core, rank


def taps():
    d = np.arange(TAPS, dtype=np.float32) - REACH
    angle = np.float32(math.pi) * d * d / TAPS
    scale = np.float32(1.0 / math.sqrt(TAPS))
    return np.cos(angle) * scale, np.sin(angle) * scale


def band(inside, outside, shift):
    at = np.arange(inside)[:, None] - np.arange(outside)[None, :] + shift
    valid = (at >= 0) & (at < TAPS)
    at = np.clip(at, 0, TAPS - 1)
    return tuple(np.where(valid, part[at], np.float32(0.0)) for part in taps())


def column_weights():
    def packed(re, im):
        return np.block([[re, im], [-im, re]])

    middle = band(LANES, LANES, REACH)
    left = band(LANES, LANES, REACH - LANES)
    right = band(LANES, LANES, REACH + LANES)
    return np.concatenate([packed(*middle), packed(left[0] + right[0], left[1] + right[1])])


def row_weights(s):
    re, im = (part.T for part in band(IN_ROWS[s], IN_ROWS[s] - 2 * REACH, 0))
    return np.block([[re, -im], [im, re]])


def polynomial(func, degree):
    w = 0.5 * (1.0 + np.cos(np.pi * (np.arange(64) + 0.5) / 64))
    fit = np.polynomial.chebyshev.Chebyshev.fit(w, func(1.5 * np.sqrt(w)), degree, domain=[0.0, 1.0])
    return [float(c) for c in fit.convert(kind=np.polynomial.Polynomial).coef]


EVEN = polynomial(lambda x: math.sqrt(2.0) * np.cos(x), 4)
ODD = polynomial(lambda x: math.sqrt(2.0) * np.sin(x) / (x / 1.5), 4)


def horner(coefs, w):
    total = jnp.full_like(w, coefs[-1])
    for c in coefs[-2::-1]:
        total = total * w + c
    return total


def cosine_sine(tile):
    w = tile * tile
    c, s = horner(EVEN, w), horner(ODD, w) * tile
    return 1.0 - s * s, s * c


ROUNDS = (1, 2, 3, 4)


def propagated(k, s):
    return -2 * k + 1 + s, 2 * k - s


def new_blocks(call, s):
    low, high = propagated(ROUNDS[call], s)
    if call:
        low_before, high_before = propagated(ROUNDS[call - 1], s)
        if ROUNDS[call] == ZS // 2:
            return [(high_before + 1, BLOCKS + low_before - 1)]
        if low_before <= high_before:
            return [(low, low_before - 1), (high_before + 1, high)]
    return [(low, high)] if low <= high else []


def kept_blocks(call, s):
    k = ROUNDS[call]
    low, high = -2 * k + s, 2 * k + 1 - s
    return (low, low + 1, high - 1, high) if low <= high else ()


def members(runs):
    return [e for low, high in runs for e in range(low, high + 1)]


def slots_of(call, s):
    return {e: at + 1 for at, e in enumerate(members([(low - 1, high + 1) for low, high in new_blocks(call, s)]))}


def handed_on(call, s):
    kept = {e % BLOCKS: at for at, e in enumerate(kept_blocks(call - 1, s))} if call else {}
    return {e: (slot, kept[e % BLOCKS]) for e, slot in slots_of(call, s).items() if e % BLOCKS in kept}


def fresh_of(call):
    return {e: slot for e, slot in slots_of(call, 0).items() if e not in handed_on(call, 0)}


def trans_of(call, s):
    return {e: at for at, e in enumerate(members(new_blocks(call, s - 1)))}


def zs_of(call):
    wanted = set(fresh_of(call))
    for s in range(1, SLICES):
        wanted |= set(trans_of(call, s))
    return {(e // 2) % ZS for e in wanted}


def body(call, holders, where_ref, *refs):
    refs = list(refs)

    def take(n):
        taken = refs[:n]
        del refs[:n]
        return taken

    last = call == len(ROUNDS) - 1
    pieces = take(len(holders))
    (weights,), rows_band, (x_wave, y_wave) = take(1), take(SLICES), take(2)
    kept_in = take(SLICES) if call else None
    earlier_calls = [c for c in range(call) if new_blocks(c, SLICES - 1)] if last else []
    done = take(len(earlier_calls))
    (out,) = take(1) if last else (None,)
    kept_out = None if last else take(SLICES)
    made = refs.pop(0) if not last and new_blocks(call, SLICES - 1) else None
    trans, fields = take(SLICES - 1), take(SLICES)
    if last:
        made, sems = take(2)
    z0, core, lo, rank = where_ref[0], where_ref[1], where_ref[2], where_ref[3]
    sign = 1 - 2 * core
    slots = [slots_of(call, s) for s in range(SLICES)]

    def half_of(e):
        return core if e % 2 == 0 else 1 - core

    def plane_block(e):
        return 2 * lax.rem(z0 + sign * (e // 2) + 2 * ZS, ZS) + half_of(e)

    def parts_of(e):
        index = jnp.where(half_of(e) == lo, 0, 1)
        sides = set()
        for ref, entries in zip(pieces, holders):
            for number, (z_at, mine) in enumerate(entries):
                if (z_at - e // 2) % ZS == 0 and mine not in sides:
                    sides.add(mine)
                    yield ref, 2 * number + index, core if mine else 1 - core

    copies = []

    def write(block, e):
        columns = pl.ds(pl.multiple_of(plane_block(e) * LANES, LANES), LANES)
        copies.append(pltpu.make_async_copy(block, out.at[:, :, :, columns], sems.at[len(copies)]))
        copies[-1].start()

    for earlier, blocks in zip(earlier_calls, done):
        for number, e in enumerate(members(new_blocks(earlier, SLICES - 1))):
            write(blocks.at[number], e)

    for s in range(SLICES):
        fields[s][0] = jnp.zeros(fields[s].shape[1:], fields[s].dtype)
        for slot, at in handed_on(call, s).values():
            fields[s][slot] = kept_in[s][at]

    for e, at in fresh_of(call).items():
        kept = [] if last else [kept_out[0].at[k] for k, kept_e in enumerate(kept_blocks(call, 0)) if kept_e == e]
        b = plane_block(e)
        for ref, index, side in parts_of(e):
            t_re, t_im = cosine_sine(ref[index, 0 : HALF[0], :].astype(jnp.float32))
            t_re, t_im = t_re.astype(jnp.bfloat16), t_im.astype(jnp.bfloat16)
            for wv in range(2):
                rows = pl.ds(pl.multiple_of(side * HALF[0], 16), HALF[0])
                x_re, x_im = x_wave[b, wv, 0:1, :], x_wave[b, wv, 1:2, :]
                y_re, y_im = y_wave[wv, 0, rows, :], y_wave[wv, 1, rows, :]
                re = (x_re * y_re - x_im * y_im).astype(jnp.bfloat16)
                im = (x_re * y_im + x_im * y_re).astype(jnp.bfloat16)
                rows = pl.ds(pl.multiple_of(wv * IN_ROWS[0] + side * HALF[0], 16), HALF[0])
                for target in (fields[0].at[at], *kept):
                    target[rows, 0:LANES] = re * t_re - im * t_im
                    target[rows, LANES:] = re * t_im + im * t_re
    for s in range(1, SLICES):
        for e, at in trans_of(call, s).items():
            for ref, index, side in parts_of(e):
                re, im = cosine_sine(ref[index, HALF_AT[s] : HALF_AT[s] + HALF[s], :].astype(jnp.float32))
                rows = pl.ds(pl.multiple_of(side * HALF[s], 16), HALF[s])
                trans[s - 1][at, rows, 0:LANES] = re.astype(jnp.bfloat16)
                trans[s - 1][at, rows, LANES:] = im.astype(jnp.bfloat16)

    for s in range(SLICES):
        rows_in, rows_out = IN_ROWS[s], IN_ROWS[s] - 2 * REACH
        lane = lax.broadcasted_iota(jnp.int32, (2 * rows_in, 2 * LANES), 1)
        from_left = (lane & (LANES - 1)) >= LANES // 2
        blocks = members(new_blocks(call, s))
        halves = []
        for e in blocks:
            at, b = slots[s][e], plane_block(e)
            left = fields[s][jnp.where(b == 0, 0, at - sign)]
            right = fields[s][jnp.where(b == BLOCKS - 1, 0, at + sign)]
            both = jnp.concatenate([fields[s][at], jnp.where(from_left, left, right)], axis=1)
            h = jnp.dot(both, weights[...], preferred_element_type=jnp.float32).astype(jnp.bfloat16)
            re = jnp.concatenate([h[:rows_in, :LANES], h[rows_in:, :LANES]], axis=1)
            im = jnp.concatenate([h[:rows_in, LANES:], h[rows_in:, LANES:]], axis=1)
            halves.append(jnp.concatenate([re, im], axis=0))
        for number, (e, h) in enumerate(zip(blocks, halves)):
            full = jnp.dot(rows_band[s][...], h, preferred_element_type=jnp.float32)
            for wv in range(2):
                re = full[:rows_out, wv * LANES : (wv + 1) * LANES]
                im = full[rows_out:, wv * LANES : (wv + 1) * LANES]
                if s + 1 < SLICES:
                    t = trans[s].at[trans_of(call, s + 1)[e]]
                    t_re, t_im = t[:, :LANES], t[:, LANES:]
                    re, im = re.astype(jnp.bfloat16), im.astype(jnp.bfloat16)
                    re, im = re * t_re - im * t_im, re * t_im + im * t_re
                    rows = slice(wv * rows_out, (wv + 1) * rows_out)
                    targets = [fields[s + 1].at[slots[s + 1][e]]] if e in slots[s + 1] else []
                    if not last:
                        kept = kept_blocks(call, s + 1)
                        targets += [kept_out[s + 1].at[at] for at, kept_e in enumerate(kept) if kept_e == e]
                    for target in targets:
                        target[rows, 0:LANES] = re
                        target[rows, LANES:] = im
                else:
                    made[number, 0, wv] = re.astype(jnp.bfloat16)
                    made[number, 1, wv] = im.astype(jnp.bfloat16)
            if last and s + 1 == SLICES:
                write(made.at[number], e)

    for copy in copies:
        copy.wait()


def propagate(call, holders, where, pieces, constants, kept, done):
    last = call == len(ROUNDS) - 1
    vmem, anywhere = pl.BlockSpec(memory_space=pltpu.VMEM), pl.BlockSpec(memory_space=pl.ANY)
    operands = [*pieces, *constants, *kept, *(done if last else ())]
    made = len(members(new_blocks(call, SLICES - 1)))
    scratch = [pltpu.VMEM((max(1, len(trans_of(call, s))), IN_ROWS[s], 2 * LANES), jnp.bfloat16) for s in range(1, SLICES)]
    scratch += [pltpu.VMEM((len(slots_of(call, s)) + 1, 2 * IN_ROWS[s], 2 * LANES), jnp.bfloat16) for s in range(SLICES)]
    if last:
        shapes = [jax.ShapeDtypeStruct((2, 2, ROWS, NX), jnp.bfloat16)]
        scratch += [pltpu.VMEM((made, 2, 2, ROWS, LANES), jnp.bfloat16), pltpu.SemaphoreType.DMA((BLOCKS,))]
    else:
        shapes = [jax.ShapeDtypeStruct((4, 2 * n, 2 * LANES), jnp.bfloat16) for n in IN_ROWS]
        if made:
            shapes += [jax.ShapeDtypeStruct((made, 2, 2, ROWS, LANES), jnp.bfloat16)]
    return pl.pallas_call(
        functools.partial(body, call, holders),
        out_shape=shapes,
        in_specs=[pl.BlockSpec(memory_space=pltpu.SMEM)] + [vmem] * len(operands),
        out_specs=[anywhere if last else vmem] * len(shapes),
        scratch_shapes=scratch,
        compiler_params=pltpu.CompilerParams(vmem_limit_bytes=40 * 2**20),
        cost_estimate=pl.CostEstimate(flops=(7 if call else 4) * 10**9, bytes_accessed=2**20, transcendentals=0),
    )(where, *operands)


def per_device(potential, tilt_index):
    wave_at, rank = lax.axis_index("wave"), lax.axis_index("rows")
    z, lo, core = wave_at // 4, (wave_at // 2) % 2, wave_at % 2
    first = core == 0

    def by_core(mine, other):
        return jnp.concatenate([jnp.where(first, mine, other), jnp.where(first, other, mine)], axis=-1)

    pair = send(potential, to_pair)
    own = by_core(potential, send(potential, to_core))
    pair = by_core(pair, send(pair, to_core))
    rows = jnp.stack([own, pair])
    down = [rows[:, s, ROWS - HALO[s] :] for s in range(SLICES)]
    up = [rows[:, s, : HALO[s]] for s in range(SLICES)]
    halo = send(jnp.where(first, jnp.concatenate(down, axis=1), jnp.concatenate(up, axis=1)), to_rank)

    top, bottom = [], []
    for s in range(SLICES):
        piece = halo[:, sum(HALO[:s]) : sum(HALO[: s + 1])]
        top += [piece, rows[:, s, :CORE_ROWS]]
        bottom += [rows[:, s, CORE_ROWS:], piece]
    mine = jnp.where(first, jnp.concatenate(top, axis=1), jnp.concatenate(bottom, axis=1))
    other = send(mine, to_core)

    tilt_index, _ = lax.optimization_barrier((tilt_index, halo))
    y = rank * ROWS - HALO[0] + jnp.arange(IN_ROWS[0], dtype=jnp.int32)
    inside = ((y >= 0) & (y < NY)).astype(jnp.float32)
    turn_y = (tilt_index[:, 0:1] * y[None, :] % NY).astype(jnp.float32) * (2.0 * math.pi / NY)
    y_wave = jnp.stack([jnp.cos(turn_y) * inside, jnp.sin(turn_y) * inside], axis=1)
    y_wave = jnp.broadcast_to(y_wave[..., None], (*y_wave.shape, LANES))
    x = jnp.arange(NX, dtype=jnp.int32)
    turn_x = (tilt_index[:, 1:2] * x[None, :] % NX).astype(jnp.float32) * (2.0 * math.pi / NX)
    x_wave = jnp.stack([jnp.cos(turn_x), jnp.sin(turn_x)], axis=1)
    x_wave = x_wave.reshape(2, 2, BLOCKS, LANES).transpose(2, 0, 1, 3)
    constants = [jnp.asarray(column_weights(), jnp.bfloat16)]
    for s in range(SLICES):
        y = rank * ROWS - HALO[s] + REACH + jnp.arange(IN_ROWS[s] - 2 * REACH, dtype=jnp.int32)
        keep = jnp.tile((y >= 0) & (y < NY), 2)[:, None]
        constants.append(jnp.where(keep, jnp.asarray(row_weights(s), jnp.bfloat16), 0))
    constants += [x_wave, y_wave]
    where = jnp.stack([z, core, lo, rank]).astype(jnp.int32)

    held = {((0, True),): mine, ((0, False),): other}
    calls = []
    for k in range(1, ZS // 2 + 1):
        mine, other = send(mine, to_next), send(other, to_next)
        if k == 1:
            mine, other, *constants = lax.optimization_barrier((mine, other, *constants))
        if calls and k < ZS // 2:
            mine, other, _ = lax.optimization_barrier((mine, other, calls[-1][0]))
        held[((-k, True),)], held[((-k, False),)] = mine, other
        if k < ZS // 2:
            held[(k, False), (k, True)] = send(jnp.concatenate([mine, other], axis=0), to_core)
        if k in ROUNDS:
            call = ROUNDS.index(k)
            holders = tuple(key for key in held if key[0][0] % ZS in zs_of(call))
            pieces = [held[key] for key in holders]
            if k == ZS // 2:
                pieces[-1], _ = lax.optimization_barrier((pieces[-1], calls[-1][0]))
            kept = calls[-1][:SLICES] if calls else []
            done = [made[SLICES] for made in calls if len(made) > SLICES]
            calls.append(propagate(call, holders, where, pieces, constants, kept, done))
    return calls[-1][0]


def solution(mesh):
    return jax.shard_map(
        per_device,
        mesh=mesh,
        in_specs=(P(None, "rows", "wave"), P("wave", None)),
        out_specs=P(None, "wave", "rows", None),
        check_vma=False,
    )
```

```python
import functools
import math

import jax
import jax.numpy as jnp
import numpy as np
from jax import lax
from jax.experimental import pallas as pl
from jax.experimental.pallas import tpu as pltpu
from jax.sharding import PartitionSpec as P

NX = 2048
NY = 512
TAPS = 33
REACH = TAPS // 2
SLICES = 4
ROWS = 64
LANES = 128
BLOCKS = NX // LANES
ZS, WAVE, RANKS = 8, 32, 8
HALO = [REACH * (SLICES - s) for s in range(SLICES)]
IN_ROWS = [ROWS + 2 * h for h in HALO]
HALF = [n // 2 for n in IN_ROWS]
HALF_AT = [sum(HALF[:s]) for s in range(SLICES)]
HALF_ALL = sum(HALF)
BOTH = ("wave", "rows")
CORE_ROWS = ROWS // 2
HALO_ALL = sum(HALO)


def place(z, lo, core, rank):
    return ((z * 2 + lo) * 2 + core) * RANKS + rank


def send(value, target_of):
    pairs = []
    for z in range(ZS):
        for lo in range(2):
            for core in range(2):
                for rank in range(RANKS):
                    target = target_of(z, lo, core, rank)
                    if target is not None:
                        pairs.append((place(z, lo, core, rank), place(*target)))
    return lax.ppermute(value, BOTH, pairs)


def to_core(z, lo, core, rank):
    return z, lo, 1 - core, rank


def to_pair(z, lo, core, rank):
    return z, 1 - lo, core, rank


def to_rank(z, lo, core, rank):
    rank += 1 - 2 * core
    return (z, lo, core, rank) if 0 <= rank < RANKS else None


def to_next(z, lo, core, rank):
    return (z + 1 - 2 * core) % ZS, lo, core, rank


def taps():
    d = np.arange(TAPS, dtype=np.float32) - REACH
    angle = np.float32(math.pi) * d * d / TAPS
    scale = np.float32(1.0 / math.sqrt(TAPS))
    return np.cos(angle) * scale, np.sin(angle) * scale


def band(inside, outside, shift):
    at = np.arange(inside)[:, None] - np.arange(outside)[None, :] + shift
    valid = (at >= 0) & (at < TAPS)
    at = np.clip(at, 0, TAPS - 1)
    return tuple(np.where(valid, part[at], np.float32(0.0)) for part in taps())


def column_weights():
    def packed(re, im):
        return np.block([[re, im], [-im, re]])

    middle = band(LANES, LANES, REACH)
    left = band(LANES, LANES, REACH - LANES)
    right = band(LANES, LANES, REACH + LANES)
    return np.concatenate([packed(*middle), packed(left[0] + right[0], left[1] + right[1])])


def row_weights(s):
    re, im = (part.T for part in band(IN_ROWS[s], IN_ROWS[s] - 2 * REACH, 0))
    return np.block([[re, -im], [im, re]])


def polynomial(func, degree):
    w = 0.5 * (1.0 + np.cos(np.pi * (np.arange(64) + 0.5) / 64))
    fit = np.polynomial.chebyshev.Chebyshev.fit(w, func(1.5 * np.sqrt(w)), degree, domain=[0.0, 1.0])
    return [float(c) for c in fit.convert(kind=np.polynomial.Polynomial).coef]


EVEN = polynomial(lambda x: math.sqrt(2.0) * np.cos(x), 4)
ODD = polynomial(lambda x: math.sqrt(2.0) * np.sin(x) / (x / 1.5), 4)


def horner(coefs, w):
    total = jnp.full_like(w, coefs[-1])
    for c in coefs[-2::-1]:
        total = total * w + c
    return total


def cosine_sine(tile):
    w = tile * tile
    c, s = horner(EVEN, w), horner(ODD, w) * tile
    return 1.0 - s * s, s * c


ROUNDS = (1, 2, 3, 4)


def propagated(k, s):
    return -2 * k + 1 + s, 2 * k - s


def new_blocks(call, s):
    low, high = propagated(ROUNDS[call], s)
    if call:
        low_before, high_before = propagated(ROUNDS[call - 1], s)
        if ROUNDS[call] == ZS // 2:
            return [(high_before + 1, BLOCKS + low_before - 1)]
        if low_before <= high_before:
            return [(low, low_before - 1), (high_before + 1, high)]
    return [(low, high)] if low <= high else []


def kept_blocks(call, s):
    k = ROUNDS[call]
    low, high = -2 * k + s, 2 * k + 1 - s
    return (low, low + 1, high - 1, high) if low <= high else ()


def members(runs):
    return [e for low, high in runs for e in range(low, high + 1)]


def slots_of(call, s):
    return {e: at + 1 for at, e in enumerate(members([(low - 1, high + 1) for low, high in new_blocks(call, s)]))}


def handed_on(call, s):
    kept = {e % BLOCKS: at for at, e in enumerate(kept_blocks(call - 1, s))} if call else {}
    return {e: (slot, kept[e % BLOCKS]) for e, slot in slots_of(call, s).items() if e % BLOCKS in kept}


def fresh_of(call):
    return {e: slot for e, slot in slots_of(call, 0).items() if e not in handed_on(call, 0)}


def trans_of(call, s):
    return {e: at for at, e in enumerate(members(new_blocks(call, s - 1)))}


def zs_of(call):
    wanted = set(fresh_of(call))
    for s in range(1, SLICES):
        wanted |= set(trans_of(call, s))
    return {(e // 2) % ZS for e in wanted}


def body(call, holders, where_ref, *refs):
    refs = list(refs)

    def take(n):
        taken = refs[:n]
        del refs[:n]
        return taken

    last = call == len(ROUNDS) - 1
    pieces = take(len(holders))
    (weights,), rows_band, (x_wave, y_wave) = take(1), take(SLICES), take(2)
    kept_in = take(SLICES) if call else None
    earlier_calls = [c for c in range(call) if new_blocks(c, SLICES - 1)] if last else []
    done = take(len(earlier_calls))
    (out,) = take(1) if last else (None,)
    kept_out = None if last else take(SLICES)
    made = refs.pop(0) if not last and new_blocks(call, SLICES - 1) else None
    trans, fields = take(SLICES - 1), take(SLICES)
    if last:
        made, sems = take(2)
    z0, core, lo, rank = where_ref[0], where_ref[1], where_ref[2], where_ref[3]
    sign = 1 - 2 * core
    slots = [slots_of(call, s) for s in range(SLICES)]

    def half_of(e):
        return core if e % 2 == 0 else 1 - core

    def plane_block(e):
        return 2 * lax.rem(z0 + sign * (e // 2) + 2 * ZS, ZS) + half_of(e)

    def parts_of(e):
        index = jnp.where(half_of(e) == lo, 0, 1)
        sides = set()
        for ref, entries in zip(pieces, holders):
            for number, (z_at, mine) in enumerate(entries):
                if (z_at - e // 2) % ZS == 0 and mine not in sides:
                    sides.add(mine)
                    yield ref, 2 * number + index, core if mine else 1 - core

    copies = []

    def write(block, e):
        columns = pl.ds(pl.multiple_of(plane_block(e) * LANES, LANES), LANES)
        copies.append(pltpu.make_async_copy(block, out.at[:, :, :, columns], sems.at[len(copies)]))
        copies[-1].start()

    for earlier, blocks in zip(earlier_calls, done):
        for number, e in enumerate(members(new_blocks(earlier, SLICES - 1))):
            write(blocks.at[number], e)

    for s in range(SLICES):
        fields[s][0] = jnp.zeros(fields[s].shape[1:], fields[s].dtype)
        for slot, at in handed_on(call, s).values():
            fields[s][slot] = kept_in[s][at]

    for e, at in fresh_of(call).items():
        kept = [] if last else [kept_out[0].at[k] for k, kept_e in enumerate(kept_blocks(call, 0)) if kept_e == e]
        b = plane_block(e)
        for ref, index, side in parts_of(e):
            t_re, t_im = cosine_sine(ref[index, 0 : HALF[0], :].astype(jnp.float32))
            t_re, t_im = t_re.astype(jnp.bfloat16), t_im.astype(jnp.bfloat16)
            for wv in range(2):
                rows = pl.ds(pl.multiple_of(side * HALF[0], 16), HALF[0])
                x_re, x_im = x_wave[b, wv, 0:1, :], x_wave[b, wv, 1:2, :]
                y_re, y_im = y_wave[wv, 0, rows, :], y_wave[wv, 1, rows, :]
                re = (x_re * y_re - x_im * y_im).astype(jnp.bfloat16)
                im = (x_re * y_im + x_im * y_re).astype(jnp.bfloat16)
                rows = pl.ds(pl.multiple_of(wv * IN_ROWS[0] + side * HALF[0], 16), HALF[0])
                for target in (fields[0].at[at], *kept):
                    target[rows, 0:LANES] = re * t_re - im * t_im
                    target[rows, LANES:] = re * t_im + im * t_re
    for s in range(1, SLICES):
        for e, at in trans_of(call, s).items():
            for ref, index, side in parts_of(e):
                re, im = cosine_sine(ref[index, HALF_AT[s] : HALF_AT[s] + HALF[s], :].astype(jnp.float32))
                rows = pl.ds(pl.multiple_of(side * HALF[s], 16), HALF[s])
                trans[s - 1][at, rows, 0:LANES] = re.astype(jnp.bfloat16)
                trans[s - 1][at, rows, LANES:] = im.astype(jnp.bfloat16)

    for s in range(SLICES):
        rows_in, rows_out = IN_ROWS[s], IN_ROWS[s] - 2 * REACH
        lane = lax.broadcasted_iota(jnp.int32, (2 * rows_in, 2 * LANES), 1)
        from_left = (lane & (LANES - 1)) >= LANES // 2
        blocks = members(new_blocks(call, s))
        halves = []
        for e in blocks:
            at, b = slots[s][e], plane_block(e)
            left = fields[s][jnp.where(b == 0, 0, at - sign)]
            right = fields[s][jnp.where(b == BLOCKS - 1, 0, at + sign)]
            both = jnp.concatenate([fields[s][at], jnp.where(from_left, left, right)], axis=1)
            h = jnp.dot(both, weights[...], preferred_element_type=jnp.float32).astype(jnp.bfloat16)
            re = jnp.concatenate([h[:rows_in, :LANES], h[rows_in:, :LANES]], axis=1)
            im = jnp.concatenate([h[:rows_in, LANES:], h[rows_in:, LANES:]], axis=1)
            halves.append(jnp.concatenate([re, im], axis=0))
        for number, (e, h) in enumerate(zip(blocks, halves)):
            full = jnp.dot(rows_band[s][...], h, preferred_element_type=jnp.float32)
            for wv in range(2):
                re = full[:rows_out, wv * LANES : (wv + 1) * LANES]
                im = full[rows_out:, wv * LANES : (wv + 1) * LANES]
                if s + 1 < SLICES:
                    t = trans[s].at[trans_of(call, s + 1)[e]]
                    t_re, t_im = t[:, :LANES], t[:, LANES:]
                    re, im = re.astype(jnp.bfloat16), im.astype(jnp.bfloat16)
                    re, im = re * t_re - im * t_im, re * t_im + im * t_re
                    rows = slice(wv * rows_out, (wv + 1) * rows_out)
                    targets = [fields[s + 1].at[slots[s + 1][e]]] if e in slots[s + 1] else []
                    if not last:
                        kept = kept_blocks(call, s + 1)
                        targets += [kept_out[s + 1].at[at] for at, kept_e in enumerate(kept) if kept_e == e]
                    for target in targets:
                        target[rows, 0:LANES] = re
                        target[rows, LANES:] = im
                else:
                    made[number, 0, wv] = re.astype(jnp.bfloat16)
                    made[number, 1, wv] = im.astype(jnp.bfloat16)
            if last and s + 1 == SLICES:
                write(made.at[number], e)

    for copy in copies:
        copy.wait()


def propagate(call, holders, where, pieces, constants, kept, done):
    last = call == len(ROUNDS) - 1
    vmem, anywhere = pl.BlockSpec(memory_space=pltpu.VMEM), pl.BlockSpec(memory_space=pl.ANY)
    operands = [*pieces, *constants, *kept, *(done if last else ())]
    made = len(members(new_blocks(call, SLICES - 1)))
    scratch = [pltpu.VMEM((max(1, len(trans_of(call, s))), IN_ROWS[s], 2 * LANES), jnp.bfloat16) for s in range(1, SLICES)]
    scratch += [pltpu.VMEM((len(slots_of(call, s)) + 1, 2 * IN_ROWS[s], 2 * LANES), jnp.bfloat16) for s in range(SLICES)]
    if last:
        shapes = [jax.ShapeDtypeStruct((2, 2, ROWS, NX), jnp.bfloat16)]
        scratch += [pltpu.VMEM((made, 2, 2, ROWS, LANES), jnp.bfloat16), pltpu.SemaphoreType.DMA((BLOCKS,))]
    else:
        shapes = [jax.ShapeDtypeStruct((4, 2 * n, 2 * LANES), jnp.bfloat16) for n in IN_ROWS]
        if made:
            shapes += [jax.ShapeDtypeStruct((made, 2, 2, ROWS, LANES), jnp.bfloat16)]
    return pl.pallas_call(
        functools.partial(body, call, holders),
        out_shape=shapes,
        in_specs=[pl.BlockSpec(memory_space=pltpu.SMEM)] + [vmem] * len(operands),
        out_specs=[anywhere if last else vmem] * len(shapes),
        scratch_shapes=scratch,
        compiler_params=pltpu.CompilerParams(vmem_limit_bytes=40 * 2**20),
        cost_estimate=pl.CostEstimate(flops=(7 if call else 4) * 10**9, bytes_accessed=2**20, transcendentals=0),
    )(where, *operands)


def per_device(potential, tilt_index):
    wave_at, rank = lax.axis_index("wave"), lax.axis_index("rows")
    z, lo, core = wave_at // 4, (wave_at // 2) % 2, wave_at % 2
    first = core == 0

    def by_core(mine, other):
        return jnp.concatenate([jnp.where(first, mine, other), jnp.where(first, other, mine)], axis=-1)

    pair = send(potential, to_pair)
    own = by_core(potential, send(potential, to_core))
    pair = by_core(pair, send(pair, to_core))
    rows = jnp.stack([own, pair])
    down = [rows[:, s, ROWS - HALO[s] :] for s in range(SLICES)]
    up = [rows[:, s, : HALO[s]] for s in range(SLICES)]
    halo = send(jnp.where(first, jnp.concatenate(down, axis=1), jnp.concatenate(up, axis=1)), to_rank)

    top, bottom = [], []
    for s in range(SLICES):
        piece = halo[:, sum(HALO[:s]) : sum(HALO[: s + 1])]
        top += [piece, rows[:, s, :CORE_ROWS]]
        bottom += [rows[:, s, CORE_ROWS:], piece]
    mine = jnp.where(first, jnp.concatenate(top, axis=1), jnp.concatenate(bottom, axis=1))
    other = send(mine, to_core)

    tilt_index, late_rank, _ = lax.optimization_barrier((tilt_index, rank, halo))
    y = late_rank * ROWS - HALO[0] + jnp.arange(IN_ROWS[0], dtype=jnp.int32)
    inside = ((y >= 0) & (y < NY)).astype(jnp.float32)
    turn_y = (tilt_index[:, 0:1] * y[None, :] % NY).astype(jnp.float32) * (2.0 * math.pi / NY)
    y_wave = jnp.stack([jnp.cos(turn_y) * inside, jnp.sin(turn_y) * inside], axis=1)
    y_wave = jnp.broadcast_to(y_wave[..., None], (*y_wave.shape, LANES))
    x = jnp.arange(NX, dtype=jnp.int32)
    turn_x = (tilt_index[:, 1:2] * x[None, :] % NX).astype(jnp.float32) * (2.0 * math.pi / NX)
    x_wave = jnp.stack([jnp.cos(turn_x), jnp.sin(turn_x)], axis=1)
    x_wave = x_wave.reshape(2, 2, BLOCKS, LANES).transpose(2, 0, 1, 3)
    constants = [jnp.asarray(column_weights(), jnp.bfloat16)]
    for s in range(SLICES):
        y = late_rank * ROWS - HALO[s] + REACH + jnp.arange(IN_ROWS[s] - 2 * REACH, dtype=jnp.int32)
        keep = jnp.tile((y >= 0) & (y < NY), 2)[:, None]
        constants.append(jnp.where(keep, jnp.asarray(row_weights(s), jnp.bfloat16), 0))
    constants += [x_wave, y_wave]
    where = jnp.stack([z, core, lo, rank]).astype(jnp.int32)

    held = {((0, True),): mine, ((0, False),): other}
    calls = []
    for k in range(1, ZS // 2 + 1):
        mine, other = send(mine, to_next), send(other, to_next)
        if k == 1:
            mine, other, *constants = lax.optimization_barrier((mine, other, *constants))
        if calls and k < ZS // 2:
            mine, other, _ = lax.optimization_barrier((mine, other, calls[-1][0]))
        held[((-k, True),)], held[((-k, False),)] = mine, other
        if k < ZS // 2:
            held[(k, False), (k, True)] = send(jnp.concatenate([mine, other], axis=0), to_core)
        if k in ROUNDS:
            call = ROUNDS.index(k)
            holders = tuple(key for key in held if key[0][0] % ZS in zs_of(call))
            pieces = [held[key] for key in holders]
            if k == ZS // 2:
                pieces[-1], _ = lax.optimization_barrier((pieces[-1], calls[-1][0]))
            kept = calls[-1][:SLICES] if calls else []
            done = [made[SLICES] for made in calls if len(made) > SLICES]
            calls.append(propagate(call, holders, where, pieces, constants, kept, done))
    return calls[-1][0]


def solution(mesh):
    return jax.shard_map(
        per_device,
        mesh=mesh,
        in_specs=(P(None, "rows", "wave"), P("wave", None)),
        out_specs=P(None, "wave", "rows", None),
        check_vma=False,
    )
```

```python
import functools
import math

import jax
import jax.numpy as jnp
import numpy as np
from jax import lax
from jax.experimental import pallas as pl
from jax.experimental.pallas import tpu as pltpu
from jax.sharding import PartitionSpec as P

NX = 2048
NY = 512
TAPS = 33
REACH = TAPS // 2
SLICES = 4
ROWS = 64
LANES = 128
BLOCKS = NX // LANES
ZS, WAVE, RANKS = 8, 32, 8
HALO = [REACH * (SLICES - s) for s in range(SLICES)]
IN_ROWS = [ROWS + 2 * h for h in HALO]
HALF = [n // 2 for n in IN_ROWS]
HALF_AT = [sum(HALF[:s]) for s in range(SLICES)]
HALF_ALL = sum(HALF)
BOTH = ("wave", "rows")
CORE_ROWS = ROWS // 2
HALO_ALL = sum(HALO)


def place(z, lo, core, rank):
    return ((z * 2 + lo) * 2 + core) * RANKS + rank


def send(value, target_of):
    pairs = []
    for z in range(ZS):
        for lo in range(2):
            for core in range(2):
                for rank in range(RANKS):
                    target = target_of(z, lo, core, rank)
                    if target is not None:
                        pairs.append((place(z, lo, core, rank), place(*target)))
    return lax.ppermute(value, BOTH, pairs)


def to_core(z, lo, core, rank):
    return z, lo, 1 - core, rank


def to_pair(z, lo, core, rank):
    return z, 1 - lo, core, rank


def to_rank(z, lo, core, rank):
    rank += 1 - 2 * core
    return (z, lo, core, rank) if 0 <= rank < RANKS else None


def to_next(z, lo, core, rank):
    return (z + 1 - 2 * core) % ZS, lo, core, rank


def taps():
    d = np.arange(TAPS, dtype=np.float32) - REACH
    angle = np.float32(math.pi) * d * d / TAPS
    scale = np.float32(1.0 / math.sqrt(TAPS))
    return np.cos(angle) * scale, np.sin(angle) * scale


def band(inside, outside, shift):
    at = np.arange(inside)[:, None] - np.arange(outside)[None, :] + shift
    valid = (at >= 0) & (at < TAPS)
    at = np.clip(at, 0, TAPS - 1)
    return tuple(np.where(valid, part[at], np.float32(0.0)) for part in taps())


def column_weights():
    def packed(re, im):
        return np.block([[re, im], [-im, re]])

    middle = band(LANES, LANES, REACH)
    left = band(LANES, LANES, REACH - LANES)
    right = band(LANES, LANES, REACH + LANES)
    return np.concatenate([packed(*middle), packed(left[0] + right[0], left[1] + right[1])])


def row_weights(s):
    re, im = (part.T for part in band(IN_ROWS[s], IN_ROWS[s] - 2 * REACH, 0))
    return np.block([[re, -im], [im, re]])


def polynomial(func, degree):
    w = 0.5 * (1.0 + np.cos(np.pi * (np.arange(64) + 0.5) / 64))
    fit = np.polynomial.chebyshev.Chebyshev.fit(w, func(1.5 * np.sqrt(w)), degree, domain=[0.0, 1.0])
    return [float(c) for c in fit.convert(kind=np.polynomial.Polynomial).coef]


EVEN = polynomial(lambda x: math.sqrt(2.0) * np.cos(x), 4)
ODD = polynomial(lambda x: math.sqrt(2.0) * np.sin(x) / (x / 1.5), 4)


def horner(coefs, w):
    total = jnp.full_like(w, coefs[-1])
    for c in coefs[-2::-1]:
        total = total * w + c
    return total


def cosine_sine(tile):
    w = tile * tile
    c, s = horner(EVEN, w), horner(ODD, w) * tile
    return 1.0 - s * s, s * c


ROUNDS = (1, 2, 3, 4)


def propagated(k, s):
    return -2 * k + 1 + s, 2 * k - s


def new_blocks(call, s):
    low, high = propagated(ROUNDS[call], s)
    if call:
        low_before, high_before = propagated(ROUNDS[call - 1], s)
        if ROUNDS[call] == ZS // 2:
            return [(high_before + 1, BLOCKS + low_before - 1)]
        if low_before <= high_before:
            return [(low, low_before - 1), (high_before + 1, high)]
    return [(low, high)] if low <= high else []


def kept_blocks(call, s):
    k = ROUNDS[call]
    low, high = -2 * k + s, 2 * k + 1 - s
    return (low, low + 1, high - 1, high) if low <= high else ()


def members(runs):
    return [e for low, high in runs for e in range(low, high + 1)]


def slots_of(call, s):
    return {e: at + 1 for at, e in enumerate(members([(low - 1, high + 1) for low, high in new_blocks(call, s)]))}


def handed_on(call, s):
    kept = {e % BLOCKS: at for at, e in enumerate(kept_blocks(call - 1, s))} if call else {}
    return {e: (slot, kept[e % BLOCKS]) for e, slot in slots_of(call, s).items() if e % BLOCKS in kept}


def fresh_of(call):
    return {e: slot for e, slot in slots_of(call, 0).items() if e not in handed_on(call, 0)}


def trans_of(call, s):
    return {e: at for at, e in enumerate(members(new_blocks(call, s - 1)))}


def zs_of(call):
    wanted = set(fresh_of(call))
    for s in range(1, SLICES):
        wanted |= set(trans_of(call, s))
    return {(e // 2) % ZS for e in wanted}


def body(call, holders, where_ref, *refs):
    refs = list(refs)

    def take(n):
        taken = refs[:n]
        del refs[:n]
        return taken

    last = call == len(ROUNDS) - 1
    pieces = take(len(holders))
    (weights,), rows_band, (x_wave, y_wave) = take(1), take(SLICES), take(2)
    kept_in = take(SLICES) if call else None
    earlier_calls = [c for c in range(call) if new_blocks(c, SLICES - 1)] if last else []
    done = take(len(earlier_calls))
    (out,) = take(1) if last else (None,)
    kept_out = None if last else take(SLICES)
    made = refs.pop(0) if not last and new_blocks(call, SLICES - 1) else None
    trans, fields = take(SLICES - 1), take(SLICES)
    if last:
        made, sems = take(2)
    z0, core, lo, rank = where_ref[0], where_ref[1], where_ref[2], where_ref[3]
    sign = 1 - 2 * core
    slots = [slots_of(call, s) for s in range(SLICES)]

    def half_of(e):
        return core if e % 2 == 0 else 1 - core

    def plane_block(e):
        return 2 * lax.rem(z0 + sign * (e // 2) + 2 * ZS, ZS) + half_of(e)

    def parts_of(e):
        index = jnp.where(half_of(e) == lo, 0, 1)
        sides = set()
        for ref, entries in zip(pieces, holders):
            for number, (z_at, mine) in enumerate(entries):
                if (z_at - e // 2) % ZS == 0 and mine not in sides:
                    sides.add(mine)
                    yield ref, 2 * number + index, core if mine else 1 - core

    copies = []

    def write(block, e):
        columns = pl.ds(pl.multiple_of(plane_block(e) * LANES, LANES), LANES)
        copies.append(pltpu.make_async_copy(block, out.at[:, :, :, columns], sems.at[len(copies)]))
        copies[-1].start()

    for earlier, blocks in zip(earlier_calls, done):
        for number, e in enumerate(members(new_blocks(earlier, SLICES - 1))):
            write(blocks.at[number], e)

    for s in range(SLICES):
        fields[s][0] = jnp.zeros(fields[s].shape[1:], fields[s].dtype)
        for slot, at in handed_on(call, s).values():
            fields[s][slot] = kept_in[s][at]

    for e, at in fresh_of(call).items():
        kept = [] if last else [kept_out[0].at[k] for k, kept_e in enumerate(kept_blocks(call, 0)) if kept_e == e]
        b = plane_block(e)
        for ref, index, side in parts_of(e):
            t_re, t_im = cosine_sine(ref[index, 0 : HALF[0], :].astype(jnp.float32))
            t_re, t_im = t_re.astype(jnp.bfloat16), t_im.astype(jnp.bfloat16)
            for wv in range(2):
                rows = pl.ds(pl.multiple_of(side * HALF[0], 16), HALF[0])
                x_re, x_im = x_wave[b, wv, 0:1, :], x_wave[b, wv, 1:2, :]
                y_re, y_im = y_wave[wv, 0, rows, :], y_wave[wv, 1, rows, :]
                re = (x_re * y_re - x_im * y_im).astype(jnp.bfloat16)
                im = (x_re * y_im + x_im * y_re).astype(jnp.bfloat16)
                rows = pl.ds(pl.multiple_of(wv * IN_ROWS[0] + side * HALF[0], 16), HALF[0])
                for target in (fields[0].at[at], *kept):
                    target[rows, 0:LANES] = re * t_re - im * t_im
                    target[rows, LANES:] = re * t_im + im * t_re
    for s in range(1, SLICES):
        for e, at in trans_of(call, s).items():
            for ref, index, side in parts_of(e):
                re, im = cosine_sine(ref[index, HALF_AT[s] : HALF_AT[s] + HALF[s], :].astype(jnp.float32))
                rows = pl.ds(pl.multiple_of(side * HALF[s], 16), HALF[s])
                trans[s - 1][at, rows, 0:LANES] = re.astype(jnp.bfloat16)
                trans[s - 1][at, rows, LANES:] = im.astype(jnp.bfloat16)

    for s in range(SLICES):
        rows_in, rows_out = IN_ROWS[s], IN_ROWS[s] - 2 * REACH
        lane = lax.broadcasted_iota(jnp.int32, (2 * rows_in, 2 * LANES), 1)
        from_left = (lane & (LANES - 1)) >= LANES // 2
        blocks = members(new_blocks(call, s))
        halves = []
        for e in blocks:
            at, b = slots[s][e], plane_block(e)
            left = fields[s][jnp.where(b == 0, 0, at - sign)]
            right = fields[s][jnp.where(b == BLOCKS - 1, 0, at + sign)]
            both = jnp.concatenate([fields[s][at], jnp.where(from_left, left, right)], axis=1)
            h = jnp.dot(both, weights[...], preferred_element_type=jnp.float32).astype(jnp.bfloat16)
            re = jnp.concatenate([h[:rows_in, :LANES], h[rows_in:, :LANES]], axis=1)
            im = jnp.concatenate([h[:rows_in, LANES:], h[rows_in:, LANES:]], axis=1)
            halves.append(jnp.concatenate([re, im], axis=0))
        for number, (e, h) in enumerate(zip(blocks, halves)):
            full = jnp.dot(rows_band[s][...], h, preferred_element_type=jnp.float32)
            for wv in range(2):
                re = full[:rows_out, wv * LANES : (wv + 1) * LANES]
                im = full[rows_out:, wv * LANES : (wv + 1) * LANES]
                if s + 1 < SLICES:
                    t = trans[s].at[trans_of(call, s + 1)[e]]
                    t_re, t_im = t[:, :LANES], t[:, LANES:]
                    re, im = re.astype(jnp.bfloat16), im.astype(jnp.bfloat16)
                    re, im = re * t_re - im * t_im, re * t_im + im * t_re
                    rows = slice(wv * rows_out, (wv + 1) * rows_out)
                    targets = [fields[s + 1].at[slots[s + 1][e]]] if e in slots[s + 1] else []
                    if not last:
                        kept = kept_blocks(call, s + 1)
                        targets += [kept_out[s + 1].at[at] for at, kept_e in enumerate(kept) if kept_e == e]
                    for target in targets:
                        target[rows, 0:LANES] = re
                        target[rows, LANES:] = im
                else:
                    made[number, 0, wv] = re.astype(jnp.bfloat16)
                    made[number, 1, wv] = im.astype(jnp.bfloat16)
            if last and s + 1 == SLICES:
                write(made.at[number], e)

    for copy in copies:
        copy.wait()


def propagate(call, holders, where, pieces, constants, kept, done):
    last = call == len(ROUNDS) - 1
    vmem, anywhere = pl.BlockSpec(memory_space=pltpu.VMEM), pl.BlockSpec(memory_space=pl.ANY)
    operands = [*pieces, *constants, *kept, *(done if last else ())]
    made = len(members(new_blocks(call, SLICES - 1)))
    scratch = [pltpu.VMEM((max(1, len(trans_of(call, s))), IN_ROWS[s], 2 * LANES), jnp.bfloat16) for s in range(1, SLICES)]
    scratch += [pltpu.VMEM((len(slots_of(call, s)) + 1, 2 * IN_ROWS[s], 2 * LANES), jnp.bfloat16) for s in range(SLICES)]
    if last:
        shapes = [jax.ShapeDtypeStruct((2, 2, ROWS, NX), jnp.bfloat16)]
        scratch += [pltpu.VMEM((made, 2, 2, ROWS, LANES), jnp.bfloat16), pltpu.SemaphoreType.DMA((BLOCKS,))]
    else:
        shapes = [jax.ShapeDtypeStruct((4, 2 * n, 2 * LANES), jnp.bfloat16) for n in IN_ROWS]
        if made:
            shapes += [jax.ShapeDtypeStruct((made, 2, 2, ROWS, LANES), jnp.bfloat16)]
    return pl.pallas_call(
        functools.partial(body, call, holders),
        out_shape=shapes,
        in_specs=[pl.BlockSpec(memory_space=pltpu.SMEM)] + [vmem] * len(operands),
        out_specs=[anywhere if last else vmem] * len(shapes),
        scratch_shapes=scratch,
        compiler_params=pltpu.CompilerParams(vmem_limit_bytes=40 * 2**20),
        cost_estimate=pl.CostEstimate(flops=(7 if call else 4) * 10**9, bytes_accessed=2**20, transcendentals=0),
    )(where, *operands)


def per_device(potential, tilt_index):
    wave_at, rank = lax.axis_index("wave"), lax.axis_index("rows")
    z, lo, core = wave_at // 4, (wave_at // 2) % 2, wave_at % 2
    first = core == 0

    def by_core(mine, other):
        return jnp.concatenate([jnp.where(first, mine, other), jnp.where(first, other, mine)], axis=-1)

    pair = send(potential, to_pair)
    own = by_core(potential, send(potential, to_core))
    pair = by_core(pair, send(pair, to_core))
    rows = jnp.stack([own, pair])
    down = [rows[:, s, ROWS - HALO[s] :] for s in range(SLICES)]
    up = [rows[:, s, : HALO[s]] for s in range(SLICES)]
    halo = send(jnp.where(first, jnp.concatenate(down, axis=1), jnp.concatenate(up, axis=1)), to_rank)

    top, bottom = [], []
    for s in range(SLICES):
        piece = halo[:, sum(HALO[:s]) : sum(HALO[: s + 1])]
        top += [piece, rows[:, s, :CORE_ROWS]]
        bottom += [rows[:, s, CORE_ROWS:], piece]
    mine = jnp.where(first, jnp.concatenate(top, axis=1), jnp.concatenate(bottom, axis=1))
    other = send(mine, to_core)

    tilt_index, _ = lax.optimization_barrier((tilt_index, rows))
    y = rank * ROWS - HALO[0] + jnp.arange(IN_ROWS[0], dtype=jnp.int32)
    inside = ((y >= 0) & (y < NY)).astype(jnp.float32)
    turn_y = (tilt_index[:, 0:1] * y[None, :] % NY).astype(jnp.float32) * (2.0 * math.pi / NY)
    y_wave = jnp.stack([jnp.cos(turn_y) * inside, jnp.sin(turn_y) * inside], axis=1)
    y_wave = jnp.broadcast_to(y_wave[..., None], (*y_wave.shape, LANES))
    x = jnp.arange(NX, dtype=jnp.int32)
    turn_x = (tilt_index[:, 1:2] * x[None, :] % NX).astype(jnp.float32) * (2.0 * math.pi / NX)
    x_wave = jnp.stack([jnp.cos(turn_x), jnp.sin(turn_x)], axis=1)
    x_wave = x_wave.reshape(2, 2, BLOCKS, LANES).transpose(2, 0, 1, 3)
    constants = [jnp.asarray(column_weights(), jnp.bfloat16)]
    for s in range(SLICES):
        y = rank * ROWS - HALO[s] + REACH + jnp.arange(IN_ROWS[s] - 2 * REACH, dtype=jnp.int32)
        keep = jnp.tile((y >= 0) & (y < NY), 2)[:, None]
        constants.append(jnp.where(keep, jnp.asarray(row_weights(s), jnp.bfloat16), 0))
    constants += [x_wave, y_wave]
    where = jnp.stack([z, core, lo, rank]).astype(jnp.int32)

    held = {((0, True),): mine, ((0, False),): other}
    calls = []
    for k in range(1, ZS // 2 + 1):
        mine, other = send(mine, to_next), send(other, to_next)
        if k == 1:
            mine, other, *constants = lax.optimization_barrier((mine, other, *constants))
        if calls and k < ZS // 2:
            mine, other, _ = lax.optimization_barrier((mine, other, calls[-1][0]))
        held[((-k, True),)], held[((-k, False),)] = mine, other
        if k < ZS // 2:
            held[(k, False), (k, True)] = send(jnp.concatenate([mine, other], axis=0), to_core)
        if k in ROUNDS:
            call = ROUNDS.index(k)
            holders = tuple(key for key in held if key[0][0] % ZS in zs_of(call))
            pieces = [held[key] for key in holders]
            if k == ZS // 2:
                pieces[-1], _ = lax.optimization_barrier((pieces[-1], calls[-1][0]))
            kept = calls[-1][:SLICES] if calls else []
            done = [made[SLICES] for made in calls if len(made) > SLICES]
            calls.append(propagate(call, holders, where, pieces, constants, kept, done))
    return calls[-1][0]


def solution(mesh):
    return jax.shard_map(
        per_device,
        mesh=mesh,
        in_specs=(P(None, "rows", "wave"), P("wave", None)),
        out_specs=P(None, "wave", "rows", None),
        check_vma=False,
    )
```
